256 devices in a mesh: pack: 32 (over y, x, core), dp: 8 (over z).
Axes of the slice: x: 4, y: 4, z: 8, core: 2. Of those that a mesh axis runs over, the one named last changes fastest.
Arguments:
- queries: bfloat16 [65536, 1024], P(('dp', 'pack')), parts along dimension 0, may hold values from -16 to 16
- keys: bfloat16 [65536, 1024], P(('dp', 'pack')), parts along dimension 0, may hold values from -16 to 16
- values: bfloat16 [65536, 1024], P(('dp', 'pack')), parts along dimension 0, may hold values from -24 to 24
- residual: bfloat16 [65536, 1024], P(('dp', 'pack')), parts along dimension 0, may hold values from -6 to 6
- segments: int32 [65536], P(('dp', 'pack')), parts along dimension 0, may hold values from 0 to 31, never falling along the last dimension, each value on 1 to 512 neighbouring positions
- out_weight: bfloat16 [1024, 1024], replicated, may hold values from -0.1875 to 0.1875
- norm_gain: float32 [1024], replicated, may hold values from 0.25 to 1.75
- routes: int32 [65536, 1], P(('dp', 'pack')), parts along dimension 0, may hold values from 0 to 31; in each aligned block of 256 rows (0 to 255, 256 to 511, ...) at most 16 rows name the same one
- gate_prob: float32 [65536], P(('dp', 'pack')), parts along dimension 0, may hold values from 0.2 to 1
- expert_in: bfloat16 [32, 1024, 2048], P('pack'), may hold values from -0.1875 to 0.1875
- expert_out: bfloat16 [32, 2048, 1024], P('pack'), may hold values from -0.125 to 0.125
Outputs:
- layer_out: bfloat16 [65536, 1024], P(('dp', 'pack')), parts along dimension 0
The draws below stay inside these ranges and needn't reach their ends.
There are 8 independent parts, one for each index of `dp`. The reference program is written for one: setup_inputs(seed, part) draws one part's arguments, and reference() takes and returns one part's arrays. A program takes and returns all parts, laid end to end along the dimension named above; an argument that names none is the same for every part. Nothing has to cross between parts.
Inputs may be any that keep to these rules, and one draw needn't show every extreme that they name: `segments`: segment numbers never fall along the pack; each image covers 1 to 512 patches, one exactly 512. `routes`: among one device's 256 patches no expert is named more than 16 times; some device names some expert exactly 16 times.
All inputs are finite; a program needn't handle non-finite values.
Results may differ from the reference program's by a relative error of at most 0.0051.
Values may be sent and summed in bfloat16 or wider, within the bound.
A program may use at most 128 MiB of HBM per device.

```python
import math
import jax
import jax.numpy as jnp
import numpy as np
from jax import lax

D = 1024
HEADS = 16
FFH = 2048
EXPERTS = 32
TOK_DEV = 256
MAXLEN = 512
TOKENS = 8192
CAP = 16
N_PACK = 32


def draw_queries(key, part):
    key = jax.random.fold_in(key, 3)
    return jnp.clip(jax.random.normal(key, (TOKENS, D), jnp.float32), -16.0, 16.0).astype(jnp.bfloat16)


def draw_keys(key, part):
    key = jax.random.fold_in(key, 4)
    return jnp.clip(jax.random.normal(key, (TOKENS, D), jnp.float32), -16.0, 16.0).astype(jnp.bfloat16)


def levels(key, shape, split, smallest, high):
    def one(dim, shards_of):
        heights = jax.random.uniform(jax.random.fold_in(jax.random.fold_in(key, 6), dim), (shards_of,), jnp.float32, smallest / len(split), high / len(split))
        return jnp.repeat(jnp.exp(heights), shape[dim] // shards_of).reshape((-1,) + (1,) * (len(shape) - dim - 1))

    factor_of = one(*split[0])
    for cut in split[1:]:
        factor_of = factor_of * one(*cut)
    return factor_of


def split_up(number_of, total, reach, lean):
    weights = [(1 << 20) // math.isqrt(grade ** lean) + 1 for grade in range(2, number_of + 1)]
    surplus, counts = total - reach - (number_of - 1), [1] * (number_of - 1)
    while surplus > 0:
        movable = [i for i in range(number_of - 1) if counts[i] < reach]
        whole, budget = sum([weights[i] for i in movable]), surplus
        for i in movable:
            more = min(reach - counts[i], max(1, budget * weights[i] // whole), surplus)
            counts[i] = counts[i] + more
            surplus = surplus - more
    return np.array([reach] + counts)


def ragged(key, number_of, total, reach, slope):
    if number_of == 2:
        one = jax.random.randint(key, (), max(1, total - reach), min(reach, total - 1) + 1)
        return jnp.stack([one, total - one])
    sizes = jnp.asarray(split_up(number_of, total, reach, slope), jnp.int32)
    twos = (number_of - 1) // 2
    source_of, taker = sizes[1:1 + 2 * twos:2], sizes[2:2 + 2 * twos:2]
    room = jnp.minimum(source_of - 1, reach - taker)
    moved = jax.random.randint(jax.random.fold_in(key, 1), (twos,), 0, 1 << 20) % (room + 1)
    sizes = sizes.at[1:1 + 2 * twos:2].set(source_of - moved).at[2:2 + 2 * twos:2].set(taker + moved)
    return sizes[jax.random.permutation(jax.random.fold_in(key, 2), number_of)]


def assign_block(stream_key, own, number, rows, number_of, top, most, lean):
    ranking = jax.random.permutation(stream_key, number_of)
    crowded, usual = shares(number_of, rows * top, most, lean, True), shares(number_of, rows * top, most, lean, False)
    places = jnp.arange(number_of)

    def named(tallies, offset_by):
        used = int((tallies > 0).sum())
        fixed = max(1, used // 4)
        moved = fixed + (places - fixed + offset_by * (used - fixed)) % max(1, number_of - fixed)
        return jnp.zeros((number_of,), jnp.int32).at[ranking[jnp.where(places < fixed, places, moved)]].set(jnp.asarray(tallies, jnp.int32))

    tallies = jnp.where(number % 4 == 0, named(crowded, number // 4), named(usual, number - number // 4 - 1))
    mixed = jax.random.permutation(jax.random.fold_in(own, 3), number_of)
    giver, taker = mixed[0:number_of // 2 * 2:2], mixed[1:number_of // 2 * 2:2]
    room = jnp.minimum(tallies[giver] - 1, most - tallies[taker]) // 2
    room = jnp.where((giver == ranking[0]) | (taker == ranking[0]) | (tallies[taker] == 0), 0, jnp.maximum(room, 0))
    moved = jax.random.randint(jax.random.fold_in(own, 4), (number_of // 2,), 0, 1 << 20) % (room + 1)
    tallies = tallies.at[giver].add(-moved).at[taker].add(moved)
    members = jnp.searchsorted(jnp.cumsum(tallies), jnp.arange(rows * top), side="right").astype(jnp.int32)
    listing = members.reshape(top, rows).T
    listing = listing[jax.random.permutation(jax.random.fold_in(own, 1), rows)]
    offset_by = jax.random.randint(jax.random.fold_in(own, 2), (rows, 1), 0, top)
    return jnp.take_along_axis(listing, (jnp.arange(top)[None, :] + offset_by) % top, axis=1)


def shares(amount, total, bound, lean, full):
    portions = [(1 << 20) // math.isqrt(rank ** lean) + 1 for rank in range(1, amount + 1)]
    largest = bound if full else min(bound, max(-(-total // amount), total * portions[0] // sum(portions)))
    least = 1 if total - largest >= amount - 1 else 0
    counts, rest = [largest] + [least] * (amount - 1), total - largest - least * (amount - 1)
    while rest > 0:
        movable = [i for i in range(1, amount) if counts[i] < largest] or [i for i in range(1, amount) if counts[i] < bound]
        pool, left = sum([portions[i] for i in movable]), rest
        for i in movable:
            more = min(bound - counts[i], max(1, left * portions[i] // pool), rest)
            counts[i] = counts[i] + more
            rest = rest - more
    return np.array(counts)


def noise(own_key, extent, width, most, cuts=(), held_as=jnp.bfloat16):
    result = width * jax.random.normal(own_key, extent, jnp.float32)
    if cuts:
        result = result * levels(own_key, extent, cuts, -0.22, 0.18)
    return jnp.clip(result, -most, most).astype(held_as)


def setup_inputs(seed: int = 0, part: int = 0) -> dict:
    arg_keys = jax.random.split(jax.random.key(seed), 12)
    part_splits = jax.random.split(jax.random.fold_in(arg_keys[11], part), 12)
    queries = draw_queries(jax.random.fold_in(jax.random.fold_in(arg_keys[11], part), 71), part)
    keys = draw_keys(jax.random.fold_in(jax.random.fold_in(arg_keys[11], part), 71), part)
    values = noise(part_splits[2], (TOKENS, D), 4.0, 24.0, ((0, 32),))
    residual = noise(part_splits[3], (TOKENS, D), 1.0, 6.0, ((0, 32),))
    segments = jnp.searchsorted(jnp.cumsum(ragged(part_splits[4], N_PACK, TOKENS, MAXLEN, 2)), jnp.arange(TOKENS), side="right").astype(jnp.int32)
    out_weight = noise(arg_keys[5], (D, D), D ** -0.5, 0.1875)
    norm_gain = jnp.clip(1.0 + 0.15 * jax.random.normal(arg_keys[6], (D,), jnp.float32), 0.25, 1.75)
    routes_keys = jax.random.split(jax.random.fold_in(part_splits[7], 1), TOKENS // TOK_DEV)
    routes_turns = jax.random.permutation(jax.random.fold_in(part_splits[7], 3), TOKENS // TOK_DEV)
    routes = jax.vmap(lambda own, number: assign_block(jax.random.fold_in(part_splits[7], 2), own, number, TOK_DEV, EXPERTS, 1, CAP, 2))(routes_keys, routes_turns).reshape((TOKENS, 1))
    gate_prob = jnp.clip(0.2 + 0.8 * jax.random.uniform(part_splits[8], (TOKENS,), jnp.float32) ** levels(part_splits[8], (TOKENS,), ((0, 32),), -0.2, 0.2), 0.2, 1.0)
    expert_in = noise(arg_keys[9], (EXPERTS, D, FFH), D ** -0.5, 0.1875, ((0, 32),))
    expert_out = noise(arg_keys[10], (EXPERTS, FFH, D), FFH ** -0.5, 0.125, ((0, 32),))
    return dict(queries=queries, keys=keys, values=values, residual=residual, segments=segments, out_weight=out_weight, norm_gain=norm_gain, routes=routes, gate_prob=gate_prob, expert_in=expert_in, expert_out=expert_out)


NEGATIVE = -1e+30

def image_attention(queries, keys, values, segments):
    row_count = TOK_DEV
    reach_count = (MAXLEN + TOK_DEV - 2) // TOK_DEV
    margin = reach_count * row_count
    head_count = HEADS
    head_width = D // HEADS
    score_scale = head_width ** (-0.5)
    marks_plus = segments + 1
    keys_padded = jnp.pad(keys, ((margin, margin), (0, 0)))
    values_padded = jnp.pad(values, ((margin, margin), (0, 0)))
    marks_padded = jnp.pad(marks_plus, (margin, margin))
    key_count = (2 * reach_count + 1) * row_count

    def one_block(block_index):
        start = (block_index * row_count).astype(jnp.int32)
        query_rows = lax.dynamic_slice_in_dim(queries, start, row_count, 0).astype(jnp.float32).reshape(row_count, head_count, head_width)
        key_rows = lax.dynamic_slice_in_dim(keys_padded, start, key_count, 0).astype(jnp.float32).reshape(key_count, head_count, head_width)
        value_rows = lax.dynamic_slice_in_dim(values_padded, start, key_count, 0).astype(jnp.float32).reshape(key_count, head_count, head_width)
        own_marks = lax.dynamic_slice_in_dim(marks_plus, start, row_count, 0)
        key_marks = lax.dynamic_slice_in_dim(marks_padded, start, key_count, 0)
        scores = jnp.einsum('qhd,khd->hqk', query_rows, key_rows) * score_scale
        same_image = own_marks[:, None] == key_marks[None, :]
        scores = jnp.where(same_image[None, :, :], scores, NEGATIVE)
        row_top = lax.optimization_barrier(jnp.max(scores, axis=2))
        exp_scores = jnp.exp(scores - row_top[:, :, None])
        row_total = lax.optimization_barrier(jnp.sum(exp_scores, axis=2))
        weights = lax.optimization_barrier(exp_scores.astype(jnp.bfloat16)).astype(jnp.float32)
        summed = jnp.einsum('hqk,khd->qhd', weights, value_rows)
        attended = summed / row_total.T[:, :, None]
        return attended.reshape(row_count, head_count * head_width).astype(jnp.bfloat16)
    blocks = lax.map(one_block, jnp.arange(N_PACK, dtype=jnp.int32))
    return blocks.reshape(N_PACK * row_count, head_count * head_width)

def expert_block(operands):
    rows_in, first_weight, second_weight = operands
    hidden = jax.nn.gelu(jnp.dot(rows_in, first_weight, preferred_element_type=jnp.float32), approximate=False).astype(jnp.bfloat16)
    return jnp.dot(hidden, second_weight, preferred_element_type=jnp.float32).astype(jnp.bfloat16)

def reference(queries, keys, values, residual, segments, out_weight, norm_gain, routes, gate_prob, expert_in, expert_out):
    attended = image_attention(queries, keys, values, segments)
    stream = residual.astype(jnp.float32) + jnp.dot(attended, out_weight, preferred_element_type=jnp.float32)
    feature_mean = lax.optimization_barrier(jnp.mean(stream, axis=1, keepdims=True))
    centered = stream - feature_mean
    feature_var = lax.optimization_barrier(jnp.mean(centered * centered, axis=1, keepdims=True))
    normed = (centered * lax.rsqrt(feature_var + 1e-06) * norm_gain).astype(jnp.bfloat16)
    expert_ids = routes[:, 0]
    onehot = (expert_ids[:, None] == jnp.arange(EXPERTS, dtype=jnp.int32)[None, :]).astype(jnp.int32)
    grouped = onehot.reshape(N_PACK, TOK_DEV, EXPERTS)
    rank_table = jnp.cumsum(grouped, axis=1) - grouped
    slot_of = lax.optimization_barrier(jnp.sum(rank_table * grouped, axis=2)).reshape(TOKENS)
    source = jnp.arange(TOKENS, dtype=jnp.int32) // TOK_DEV
    position = source * CAP + slot_of
    buffers = jnp.zeros((EXPERTS, N_PACK * CAP, D), jnp.bfloat16).at[expert_ids, position].set(normed)
    results = lax.map(expert_block, (buffers, expert_in, expert_out))
    expert_result = results[expert_ids, position]
    layer_out = stream + gate_prob[:, None] * expert_result.astype(jnp.float32)
    return layer_out.astype(jnp.bfloat16)
```

```python
import jax
import jax.numpy as jnp
from jax import lax
from jax.experimental import pallas as pl
from jax.experimental.pallas import tpu as pltpu
from jax.sharding import PartitionSpec as P

HEADS = 16
PACK = 32
SIDE = 4
ROWS = 256
CAP = 16
PAIRS = HEADS // 2
LANES = 128
FAR_AWAY = -1e30
MESH = pl.DeviceIdType.MESH
OWN, SIB, PREV, NEXT, FWD = range(5)


def hops(step):
    return min(step[0], SIDE - step[0]) + min(step[1], SIDE - step[1])


STEPS = sorted(
    [(dy, dx, dc) for dy in range(SIDE) for dx in range(SIDE) for dc in (1, 0)],
    key=lambda step: (-hops(step), step[0], step[1], -step[2]),
)
HALF = PACK // 2


def moved(me, step, sign):
    y, x, core = me // (2 * SIDE), (me // 2) % SIDE, me % 2
    y = lax.rem(y + sign * step[0] + SIDE, SIDE)
    x = lax.rem(x + sign * step[1] + SIDE, SIDE)
    core = lax.rem(core + step[2], 2)
    return (y * SIDE + x) * 2 + core


def kernel(
    q_hbm, k_hbm, v_hbm, res_hbm, seg_ref, route_ref, gate_ref, gain_ref, wo_hbm, w1_hbm, w2_hbm,
    out_ref,
    qs, kt, vt, segs, qaug, kaug, res, wo, w1, w2, stream, place, place_t, gate_cols,
    outg, recv, hid, prod, ret,
    load_sem, near_send, near_recv, seg_send, seg_recv, sib_send, sib_recv, fwd_send, fwd_recv,
    go_send, go_recv, back_send, back_recv,
):
    me = lax.axis_index("pack")
    core = lax.rem(me, 2)
    sibling = me + 1 - 2 * core
    after = lax.rem(me + 2, PACK)
    before = lax.rem(me + PACK - 2, PACK)
    fwd_from = NEXT - core

    barrier = pltpu.get_barrier_semaphore()

    @pl.loop(1, PACK)
    def _(d):
        pl.semaphore_signal(
            barrier, inc=1, device_id={"pack": lax.rem(me + d, PACK)}, device_id_type=MESH
        )

    loads = [
        pltpu.make_async_copy(src, dst, load_sem.at[i])
        for i, (src, dst) in enumerate(
            [
                (k_hbm, kt.at[OWN]),
                (v_hbm, vt.at[OWN]),
                (q_hbm, qs),
                (res_hbm, res),
                (wo_hbm, wo),
                (w1_hbm.at[0], w1),
                (w2_hbm.at[0], w2),
            ]
        )
    ]
    for load in loads[:4]:
        load.start()
    pl.semaphore_wait(barrier, PACK - 1)

    def cols(p):
        return pl.ds(pl.multiple_of(p * LANES, LANES), LANES)

    def remote(src, dst, send, recv_s, peer):
        return pltpu.make_async_remote_copy(
            src_ref=src, dst_ref=dst, send_sem=send, recv_sem=recv_s,
            device_id={"pack": peer}, device_id_type=MESH,
        )

    def halo(p):
        c = cols(p)
        return [
            remote(k_hbm.at[:, c], kt.at[PREV, :, c], near_send.at[0, p], near_recv.at[0, p], after),
            remote(v_hbm.at[:, c], vt.at[PREV, :, c], near_send.at[1, p], near_recv.at[1, p], after),
            remote(k_hbm.at[:, c], kt.at[NEXT, :, c], near_send.at[2, p], near_recv.at[2, p], before),
            remote(v_hbm.at[:, c], vt.at[NEXT, :, c], near_send.at[3, p], near_recv.at[3, p], before),
        ]

    def forward(p):
        c = cols(p)
        return [
            remote(kt.at[fwd_from, :, c], kt.at[FWD, :, c], fwd_send.at[0, p], fwd_recv.at[0, p], sibling),
            remote(vt.at[fwd_from, :, c], vt.at[FWD, :, c], fwd_send.at[1, p], fwd_recv.at[1, p], sibling),
        ]

    seg_out = [
        remote(seg_ref, segs.at[PREV], seg_send.at[0], seg_recv.at[0], after),
        remote(seg_ref, segs.at[NEXT], seg_send.at[1], seg_recv.at[1], before),
        remote(seg_ref, segs.at[SIB], seg_send.at[2], seg_recv.at[2], sibling),
    ]
    seg_fwd = remote(segs.at[fwd_from], segs.at[FWD], seg_send.at[3], seg_recv.at[3], sibling)
    sib_out = [
        remote(k_hbm, kt.at[SIB], sib_send.at[0], sib_recv.at[0], sibling),
        remote(v_hbm, vt.at[SIB], sib_send.at[1], sib_recv.at[1], sibling),
    ]
    for copy in seg_out + halo(0):
        copy.start()
    for copy in sib_out:
        copy.start()

    @pl.loop(1, PAIRS)
    def _(p):
        for copy in halo(p):
            copy.start()

    for load in loads[4:]:
        load.start()

    def image_rows(seg):
        spread = jnp.broadcast_to(seg[0:1, :], (LANES, ROWS))
        return spread == lax.broadcasted_iota(jnp.int32, (LANES, ROWS), 0)

    own_rows = image_rows(seg_ref[...])
    qaug[...] = jnp.where(own_rows, FAR_AWAY, 0.0).T.astype(jnp.bfloat16)
    kaug[OWN] = jnp.where(own_rows, 0.0, 1.0).T.astype(jnp.bfloat16)

    expert_of = jnp.zeros((PACK, ROWS), jnp.int32)
    place_iota = lax.broadcasted_iota(jnp.int32, (PACK, ROWS), 0)
    for j, step in enumerate(STEPS):
        expert_of = jnp.where(place_iota == j, moved(me, step, 1), expert_of)
    chosen = jnp.broadcast_to(route_ref[0:1, :], (PACK, ROWS)) == expert_of
    earlier = lax.broadcasted_iota(jnp.int32, (ROWS, ROWS), 0) < lax.broadcasted_iota(
        jnp.int32, (ROWS, ROWS), 1
    )
    rank = jnp.dot(
        jnp.where(chosen, 1.0, 0.0).astype(jnp.bfloat16),
        jnp.where(earlier, 1.0, 0.0).astype(jnp.bfloat16),
        preferred_element_type=jnp.float32,
    )
    slot = jnp.where(chosen, rank, -1.0)
    slot_iota = lax.broadcasted_iota(jnp.int32, (CAP, ROWS), 0).astype(jnp.float32)
    for j in range(PACK):
        hit = jnp.broadcast_to(slot[j : j + 1, :], (CAP, ROWS)) == slot_iota
        hit = jnp.where(hit, 1.0, 0.0)
        place[CAP * j : CAP * (j + 1), :] = hit.astype(jnp.bfloat16)
    for j in range(0, PACK * CAP, LANES):
        place_t[:, j : j + LANES] = place[j : j + LANES, :].astype(jnp.float32).T.astype(jnp.bfloat16)
    gate_cols[...] = jnp.broadcast_to(gate_ref[0:1, :], (LANES, ROWS)).T

    for copy in seg_out:
        copy.wait_recv()
    seg_fwd.start()
    for tile in (SIB, PREV, NEXT):
        kaug[tile] = jnp.where(image_rows(segs[tile]), 0.0, 1.0).T.astype(jnp.bfloat16)
    seg_fwd.wait_recv()
    kaug[FWD] = jnp.where(image_rows(segs[FWD]), 0.0, 1.0).T.astype(jnp.bfloat16)

    for load in loads[:5]:
        load.wait()
    stream[...] = res[...].astype(jnp.float32)
    for copy in sib_out:
        copy.wait_recv()

    exp_scale = float((1024 // HEADS) ** -0.5 * 1.4426950408889634)
    low_lanes = lax.broadcasted_iota(jnp.int32, (ROWS, LANES), 1) < LANES // 2
    ones = jnp.ones((ROWS, LANES), jnp.bfloat16)

    def attend(p):
        c = cols(p)
        both = qs[:, c]
        marks = qaug[...]
        heads = []
        for keep in (low_lanes, jnp.logical_not(low_lanes)):
            one = jnp.where(keep, both, jnp.zeros_like(both))
            lhs = jnp.concatenate([one, marks], axis=1)
            scores = []
            for tile in range(5):
                rhs = jnp.concatenate([kt[tile, :, c], kaug[tile]], axis=1)
                scores.append(
                    lax.dot_general(
                        lhs, rhs, (((1,), (1,)), ((), ())), preferred_element_type=jnp.float32
                    )
                )
            top = scores[0]
            for s in scores[1:]:
                top = jnp.maximum(top, s)
            top = jnp.max(top, axis=1, keepdims=True)
            summed = jnp.zeros((ROWS, 2 * LANES), jnp.float32)
            for tile in range(5):
                weights = jnp.exp2((scores[tile] - top) * exp_scale).astype(jnp.bfloat16)
                rhs = jnp.concatenate([vt[tile, :, c], ones], axis=1)
                summed = summed + jnp.dot(weights, rhs, preferred_element_type=jnp.float32)
            heads.append(summed[:, :LANES] / summed[:, LANES:])
        attended = jnp.where(low_lanes, heads[0], heads[1]).astype(jnp.bfloat16)
        stream[...] += jnp.dot(attended, wo[c, :], preferred_element_type=jnp.float32)

    def take(p):
        for copy in halo(p):
            copy.wait_recv()
        for copy in forward(p):
            copy.start()

    take(0)

    @pl.loop(1, PAIRS)
    def _(p):
        take(p)
        for copy in forward(p - 1):
            copy.wait_recv()
        attend(p - 1)

    for copy in forward(PAIRS - 1):
        copy.wait_recv()
    attend(PAIRS - 1)

    x = stream[...]
    mean = jnp.mean(x, axis=1, keepdims=True)
    centered = x - mean
    var = jnp.mean(centered * centered, axis=1, keepdims=True)
    normed = (centered * lax.rsqrt(var + 1e-6) * gain_ref[0:1, :]).astype(jnp.bfloat16)

    def block(j):
        return pl.ds(j * CAP, CAP)

    go = [
        remote(outg.at[block(j)], recv.at[block(j)], go_send.at[j], go_recv.at[j], moved(me, step, 1))
        for j, step in enumerate(STEPS[:-1])
    ]
    back = [
        remote(prod.at[block(j)], ret.at[block(j)], back_send.at[j], back_recv.at[j], moved(me, step, -1))
        for j, step in enumerate(STEPS[:-1])
    ]
    part = 128
    for start in range(0, PACK * CAP, part):
        outg[start : start + part, :] = jnp.dot(
            place[start : start + part, :], normed, preferred_element_type=jnp.float32
        ).astype(jnp.bfloat16)
        for j in range(start // CAP, min((start + part) // CAP, PACK - 1)):
            go[j].start()
    recv[(PACK - 1) * CAP :, :] = outg[(PACK - 1) * CAP :, :]

    loads[5].wait()
    loads[6].wait()
    wide = 512

    for half in range(2):
        rows = pl.ds(half * ROWS, ROWS)
        for j in range(half * HALF, min((half + 1) * HALF, PACK - 1)):
            go[j].wait_recv()

        @pl.loop(0, 2048 // wide)
        def _(n):
            c = pl.ds(pl.multiple_of(n * wide, wide), wide)
            h = jnp.dot(recv[rows, :], w1[:, c], preferred_element_type=jnp.float32)
            h = 0.5 * h * (1.0 + lax.erf(h * 0.7071067811865476))
            hid[:, c] = h.astype(jnp.bfloat16)

        @pl.loop(0, 1024 // wide)
        def _(n):
            c = pl.ds(pl.multiple_of(n * wide, wide), wide)
            prod[rows, c] = jnp.dot(
                hid[...], w2[:, c], preferred_element_type=jnp.float32
            ).astype(jnp.bfloat16)

        for j in range(half * HALF, min((half + 1) * HALF, PACK - 1)):
            back[j].start()
    ret[(PACK - 1) * CAP :, :] = prod[(PACK - 1) * CAP :, :]

    gate = jnp.concatenate([gate_cols[...]] * (1024 // LANES), axis=1)
    for j in range(HALF):
        back[j].wait_recv()
    first = jnp.dot(place_t[:, :ROWS], ret[:ROWS, :], preferred_element_type=jnp.float32)
    stream[...] += gate * first
    for j in range(HALF, PACK - 1):
        back[j].wait_recv()
    second = jnp.dot(place_t[:, ROWS:], ret[ROWS:, :], preferred_element_type=jnp.float32)
    out_ref[...] = (stream[...] + gate * second).astype(jnp.bfloat16)

    for copy in seg_out + sib_out + [seg_fwd]:
        copy.wait_send()

    @pl.loop(0, PAIRS)
    def _(p):
        for copy in halo(p) + forward(p):
            copy.wait_send()

    for copy in go + back:
        copy.wait_send()


def on_device(
    queries, keys, values, residual, segments, out_weight, norm_gain, routes, gate_prob,
    expert_in, expert_out,
):
    bf16, f32 = jnp.bfloat16, jnp.float32
    hbm = pl.BlockSpec(memory_space=pl.ANY)
    vmem = pl.BlockSpec(memory_space=pltpu.VMEM)
    rows_of = lambda row: jnp.broadcast_to(row.reshape(1, ROWS), (8, ROWS))
    dma = pltpu.SemaphoreType.DMA
    return pl.pallas_call(
        kernel,
        out_shape=jax.ShapeDtypeStruct((ROWS, 1024), bf16),
        in_specs=[hbm] * 4 + [vmem] * 4 + [hbm] * 3,
        out_specs=vmem,
        scratch_shapes=[
            pltpu.VMEM((ROWS, 1024), bf16),
            pltpu.VMEM((5, ROWS, 1024), bf16),
            pltpu.VMEM((5, ROWS, 1024), bf16),
            pltpu.VMEM((5, 8, ROWS), jnp.int32),
            pltpu.VMEM((ROWS, LANES), bf16),
            pltpu.VMEM((5, ROWS, LANES), bf16),
            pltpu.VMEM((ROWS, 1024), bf16),
            pltpu.VMEM((1024, 1024), bf16),
            pltpu.VMEM((1024, 2048), bf16),
            pltpu.VMEM((2048, 1024), bf16),
            pltpu.VMEM((ROWS, 1024), f32),
            pltpu.VMEM((PACK * CAP, ROWS), bf16),
            pltpu.VMEM((ROWS, PACK * CAP), bf16),
            pltpu.VMEM((ROWS, LANES), f32),
            pltpu.VMEM((PACK * CAP, 1024), bf16),
            pltpu.VMEM((PACK * CAP, 1024), bf16),
            pltpu.VMEM((ROWS, 2048), bf16),
            pltpu.VMEM((PACK * CAP, 1024), bf16),
            pltpu.VMEM((PACK * CAP, 1024), bf16),
            dma((7,)),
            dma((4, PAIRS)),
            dma((4, PAIRS)),
            dma((4,)),
            dma((4,)),
            dma((2,)),
            dma((2,)),
            dma((2, PAIRS)),
            dma((2, PAIRS)),
            dma((PACK,)),
            dma((PACK,)),
            dma((PACK,)),
            dma((PACK,)),
        ],
        compiler_params=pltpu.CompilerParams(
            collective_id=0, has_side_effects=True, vmem_limit_bytes=56 << 20
        ),
        name="layer",
    )(
        queries, keys, values, residual,
        rows_of(segments), rows_of(routes), rows_of(gate_prob),
        jnp.broadcast_to(norm_gain.reshape(1, 1024), (8, 1024)),
        out_weight, expert_in, expert_out,
    )


def solution(mesh):
    placed = (
        P(("dp", "pack"), None),
        P(("dp", "pack"), None),
        P(("dp", "pack"), None),
        P(("dp", "pack"), None),
        P(("dp", "pack")),
        P(),
        P(),
        P(("dp", "pack"), None),
        P(("dp", "pack")),
        P("pack", None, None),
        P("pack", None, None),
    )
    return jax.shard_map(
        on_device, mesh=mesh, in_specs=placed, out_specs=P(("dp", "pack"), None), check_vma=False
    )
```

```python
import jax
import jax.numpy as jnp
from jax import lax
from jax.experimental import pallas as pl
from jax.experimental.pallas import tpu as pltpu
from jax.sharding import PartitionSpec as P

HEADS = 16
PACK = 32
SIDE = 4
ROWS = 256
CAP = 16
PAIRS = HEADS // 2
LANES = 128
FAR_AWAY = -1e30
MESH = pl.DeviceIdType.MESH
OWN, SIB, NEAR, FAR, FWD = range(5)
KEPT = 5
WAVES = (0, 10, 22, 32)
WIDE = 512


def hops(step):
    return min(step[0], SIDE - step[0]) + min(step[1], SIDE - step[1])


STEPS = sorted(
    [(dy, dx, dc) for dy in range(SIDE) for dx in range(SIDE) for dc in (1, 0)],
    key=lambda step: (-hops(step), step[0], step[1], -step[2]),
)
HALF = PACK // 2


def moved(me, step, sign):
    y, x, core = me // (2 * SIDE), (me // 2) % SIDE, me % 2
    y = lax.rem(y + sign * step[0] + SIDE, SIDE)
    x = lax.rem(x + sign * step[1] + SIDE, SIDE)
    core = lax.rem(core + step[2], 2)
    return (y * SIDE + x) * 2 + core


def kernel(
    q_hbm, k_hbm, v_hbm, res_hbm, seg_ref, route_ref, gate_ref, gain_ref, wo_hbm, w1_hbm, w2_hbm,
    out_ref,
    qs, kt, vt, near, fwd, pick, help_out, help_in, segs, qaug, kaug, helped, att,
    res, wo, w1, w2, stream, place, place_t, gate_cols, outg, recv, hid, prod, ret,
    load_sem, seg_send, seg_recv, sib_send, sib_recv, near_send, near_recv, fwd_send, fwd_recv,
    help_send, help_recv, go_send, go_recv, back_send, back_recv,
):
    me = lax.axis_index("pack")
    core = lax.rem(me, 2)
    sibling = me + 1 - 2 * core
    across = lax.rem(me + 2 * core + PACK - 1, PACK)

    barrier = pltpu.get_barrier_semaphore()

    @pl.loop(1, PACK)
    def _(d):
        pl.semaphore_signal(
            barrier, inc=1, device_id={"pack": lax.rem(me + d, PACK)}, device_id_type=MESH
        )

    loads = [
        pltpu.make_async_copy(src, dst, load_sem.at[i])
        for i, (src, dst) in enumerate(
            [
                (k_hbm, kt.at[OWN]),
                (v_hbm, vt.at[OWN]),
                (q_hbm, qs),
                (res_hbm, res),
                (wo_hbm, wo),
                (w1_hbm.at[0], w1),
                (w2_hbm.at[0], w2),
            ]
        )
    ]
    for load in loads[:4]:
        load.start()
    segs[OWN] = jnp.broadcast_to(seg_ref[0:1, :], (8, ROWS))
    pl.semaphore_wait(barrier, PACK - 1)

    def cols(p):
        return pl.ds(pl.multiple_of(p * LANES, LANES), LANES)

    def remote(src, dst, send, recv_s, peer):
        return pltpu.make_async_remote_copy(
            src_ref=src, dst_ref=dst, send_sem=send, recv_sem=recv_s,
            device_id={"pack": peer}, device_id_type=MESH,
        )

    def plain(p):
        return [
            remote(hbm.at[:, cols(p)], near.at[2 * p + i], near_send.at[2 * p + i], near_recv.at[2 * p + i], across)
            for i, hbm in enumerate((k_hbm, v_hbm))
        ]

    def picked(n):
        at = 2 * KEPT + n
        return remote(pick.at[n], near.at[at], near_send.at[at], near_recv.at[at], across)

    def forward(n):
        return remote(near.at[n], fwd.at[n], fwd_send.at[n], fwd_recv.at[n], sibling)

    def helping(n):
        return remote(help_out.at[n], help_in.at[n], help_send.at[n], help_recv.at[n], across)

    seg_out = [
        remote(segs.at[OWN], segs.at[NEAR], seg_send.at[0], seg_recv.at[0], across),
        remote(segs.at[OWN], segs.at[SIB], seg_send.at[1], seg_recv.at[1], sibling),
    ]
    seg_on = [
        remote(segs.at[SIB], segs.at[FAR], seg_send.at[2], seg_recv.at[2], across),
        remote(segs.at[NEAR], segs.at[FWD], seg_send.at[3], seg_recv.at[3], sibling),
    ]
    first, rest = pl.ds(0, KEPT * LANES), pl.ds(KEPT * LANES, (PAIRS - KEPT) * LANES)
    sib_out = [
        remote(hbm.at[:, c], tile.at[SIB, :, c], sib_send.at[i, n], sib_recv.at[i, n], sibling)
        for n, c in enumerate((first, rest))
        for i, (hbm, tile) in enumerate(((k_hbm, kt), (v_hbm, vt)))
    ]
    for copy in seg_out + plain(0) + sib_out:
        copy.start()

    def edge(row, at_end):
        return jnp.where(at_end, row[:, ROWS - 1 :], row[:, :1])

    for copy in seg_out:
        copy.wait_recv()
    for copy in seg_on:
        copy.start()
    for load in loads[:4]:
        load.wait()
    for copy in sib_out[:2]:
        copy.wait_recv()
    last = core == 1
    sib_edge = edge(segs[SIB, 0:1, :], last)
    near_edge = edge(segs[NEAR, 0:1, :], core == 0)
    own_edge = edge(segs[OWN, 0:1, :], last)
    wide_here = jnp.broadcast_to(sib_edge, (ROWS, LANES)) == jnp.broadcast_to(near_edge, (ROWS, LANES))
    usual = [(t.at[OWN], p) for p in range(KEPT, PAIRS) for t in (kt, vt)]
    usual += [(qs, p) for p in range(KEPT, PAIRS)]
    for n in range(2 * KEPT):
        wide = (kt, vt)[n % 2][SIB, :, LANES * (n // 2) : LANES * (n // 2 + 1)]
        if n < len(usual):
            src, p = usual[n]
            wide = jnp.where(wide_here, wide, src[:, LANES * p : LANES * (p + 1)])
        pick[n] = wide
        picked(n).start()

    @pl.loop(1, KEPT)
    def _(p):
        for copy in plain(p):
            copy.start()

    for load in loads[4:]:
        load.start()

    def image_rows(seg):
        spread = jnp.broadcast_to(seg[0:1, :], (LANES, ROWS))
        return spread == lax.broadcasted_iota(jnp.int32, (LANES, ROWS), 0)

    def query_marks(rows):
        return jnp.where(rows, FAR_AWAY, 0.0).T.astype(jnp.bfloat16)

    def key_marks(rows):
        return jnp.where(rows, 0.0, 1.0).T.astype(jnp.bfloat16)

    own_rows, near_rows = image_rows(segs[OWN]), image_rows(segs[NEAR])
    qaug[0] = query_marks(own_rows)
    qaug[1] = query_marks(near_rows)
    kaug[OWN] = key_marks(own_rows)
    kaug[NEAR] = key_marks(near_rows)
    kaug[SIB] = key_marks(image_rows(segs[SIB]))
    for copy in seg_on:
        copy.wait_recv()
    kaug[FWD] = key_marks(image_rows(segs[FWD]))
    far_edge = edge(segs[FAR, 0:1, :], core == 0)
    wide_there = jnp.broadcast_to(far_edge, (LANES, ROWS)) == jnp.broadcast_to(own_edge, (LANES, ROWS))
    kaug[FAR] = key_marks(jnp.logical_and(wide_there, image_rows(segs[FAR])))
    in_crossing = jnp.broadcast_to(segs[OWN, 0:1, :], (LANES, ROWS)) == jnp.broadcast_to(own_edge, (LANES, ROWS))
    helped[...] = jnp.where(jnp.logical_and(wide_there, in_crossing), 1.0, 0.0).T

    expert_of = jnp.zeros((PACK, ROWS), jnp.int32)
    place_iota = lax.broadcasted_iota(jnp.int32, (PACK, ROWS), 0)
    for j, step in enumerate(STEPS):
        expert_of = jnp.where(place_iota == j, moved(me, step, 1), expert_of)
    chosen = jnp.broadcast_to(route_ref[0:1, :], (PACK, ROWS)) == expert_of
    earlier = lax.broadcasted_iota(jnp.int32, (ROWS, ROWS), 0) < lax.broadcasted_iota(
        jnp.int32, (ROWS, ROWS), 1
    )
    rank = jnp.dot(
        jnp.where(chosen, 1.0, 0.0).astype(jnp.bfloat16),
        jnp.where(earlier, 1.0, 0.0).astype(jnp.bfloat16),
        preferred_element_type=jnp.float32,
    )
    slot = jnp.where(chosen, rank, -1.0)
    slot_iota = lax.broadcasted_iota(jnp.int32, (CAP, ROWS), 0).astype(jnp.float32)
    for j in range(PACK):
        hit = jnp.broadcast_to(slot[j : j + 1, :], (CAP, ROWS)) == slot_iota
        hit = jnp.where(hit, 1.0, 0.0)
        place[CAP * j : CAP * (j + 1), :] = hit.astype(jnp.bfloat16)
    for j in range(0, PACK * CAP, LANES):
        place_t[:, j : j + LANES] = place[j : j + LANES, :].astype(jnp.float32).T.astype(jnp.bfloat16)
    gate_cols[...] = jnp.broadcast_to(gate_ref[0:1, :], (LANES, ROWS)).T
    stream[...] = res[...].astype(jnp.float32)

    exp_scale = float((1024 // HEADS) ** -0.5 * 1.4426950408889634)
    low_lanes = lax.broadcasted_iota(jnp.int32, (ROWS, LANES), 1) < LANES // 2
    ones = jnp.ones((ROWS, LANES), jnp.bfloat16)

    def two_heads(both, marks, tiles):
        heads = []
        for keep in (low_lanes, jnp.logical_not(low_lanes)):
            one = jnp.where(keep, both, jnp.zeros_like(both))
            lhs = jnp.concatenate([one, marks], axis=1)
            scores = []
            for key, mark, _ in tiles:
                rhs = jnp.concatenate([key(), mark()], axis=1)
                scores.append(
                    lax.dot_general(
                        lhs, rhs, (((1,), (1,)), ((), ())), preferred_element_type=jnp.float32
                    )
                )
            top = scores[0]
            for s in scores[1:]:
                top = jnp.maximum(top, s)
            top = jnp.max(top, axis=1, keepdims=True)
            summed = jnp.zeros((ROWS, 2 * LANES), jnp.float32)
            for s, (_, _, value) in zip(scores, tiles):
                weights = jnp.exp2((s - top) * exp_scale).astype(jnp.bfloat16)
                rhs = jnp.concatenate([value(), ones], axis=1)
                summed = summed + jnp.dot(weights, rhs, preferred_element_type=jnp.float32)
            heads.append(summed[:, :LANES] / summed[:, LANES:])
        return jnp.where(low_lanes, heads[0], heads[1]).astype(jnp.bfloat16)

    def at_home(p, place_of):
        return (lambda: kt[place_of, :, cols(p)], lambda: kaug[place_of], lambda: vt[place_of, :, cols(p)])

    def arrived(buf, at, place_of):
        return (lambda: buf[at], lambda: kaug[place_of], lambda: buf[at + 1])

    def attend(p, with_far):
        tiles = [at_home(p, OWN), at_home(p, SIB), arrived(near, 2 * p, NEAR), arrived(fwd, 2 * p, FWD)]
        if with_far:
            tiles.append(arrived(near, 2 * KEPT + 2 * p, FAR))
        return two_heads(qs[:, cols(p)], qaug[0], tiles)

    for copy in sib_out[2:]:
        copy.wait_recv()
    for copy in plain(0):
        copy.wait_recv()
    for n in range(2):
        forward(n).start()
    for n in range(2 * KEPT):
        picked(n).wait_recv()
        if n < 2 * (PAIRS - KEPT):
            forward(2 * KEPT + n).start()

    @pl.loop(KEPT, PAIRS)
    def _(p):
        tiles = [at_home(p, OWN), at_home(p, SIB), arrived(near, 2 * p, NEAR)]
        help_out[p - KEPT] = two_heads(near[2 * PAIRS + p - KEPT], qaug[1], tiles)
        helping(p - KEPT).start()

    @pl.loop(KEPT, PAIRS)
    def _(p):
        forward(2 * p).wait_recv()
        forward(2 * p + 1).wait_recv()
        att[:, cols(p)] = attend(p, False)

    loads[4].wait()

    @pl.loop(0, KEPT)
    def _(p):
        @pl.when(p < KEPT - 1)
        def _():
            for n, copy in enumerate(plain(p + 1)):
                copy.wait_recv()
                forward(2 * p + 2 + n).start()

        forward(2 * p).wait_recv()
        forward(2 * p + 1).wait_recv()
        stream[...] += jnp.dot(attend(p, True), wo[cols(p), :], preferred_element_type=jnp.float32)

    for n in range(PAIRS - KEPT):
        helping(n).wait_recv()
        c = slice((KEPT + n) * LANES, (KEPT + n + 1) * LANES)
        att[:, c] = jnp.where(helped[...] > 0.5, help_in[n], att[:, c])

    x = stream[...] + jnp.dot(
        att[:, KEPT * LANES :], wo[KEPT * LANES :, :], preferred_element_type=jnp.float32
    )
    stream[...] = x
    mean = jnp.mean(x, axis=1, keepdims=True)
    centered = x - mean
    var = jnp.mean(centered * centered, axis=1, keepdims=True)
    normed = (centered * lax.rsqrt(var + 1e-6) * gain_ref[0:1, :]).astype(jnp.bfloat16)

    def block(j):
        return pl.ds(j * CAP, CAP)

    go = [
        remote(outg.at[block(j)], recv.at[block(j)], go_send.at[j], go_recv.at[j], moved(me, step, 1))
        for j, step in enumerate(STEPS[:-1])
    ]
    back = [
        remote(prod.at[block(j)], ret.at[block(j)], back_send.at[j], back_recv.at[j], moved(me, step, -1))
        for j, step in enumerate(STEPS[:-1])
    ]
    part = 128
    for start in range(0, PACK * CAP, part):
        outg[start : start + part, :] = jnp.dot(
            place[start : start + part, :], normed, preferred_element_type=jnp.float32
        ).astype(jnp.bfloat16)
        for j in range(start // CAP, min((start + part) // CAP, PACK - 1)):
            go[j].start()
    recv[(PACK - 1) * CAP :, :] = outg[(PACK - 1) * CAP :, :]

    loads[5].wait()
    loads[6].wait()

    for begin, end in zip(WAVES, WAVES[1:]):
        rows, count = pl.ds(begin * CAP, (end - begin) * CAP), (end - begin) * CAP
        for j in range(begin, min(end, PACK - 1)):
            go[j].wait_recv()

        @pl.loop(0, 2048 // WIDE)
        def _(n):
            c = pl.ds(pl.multiple_of(n * WIDE, WIDE), WIDE)
            h = jnp.dot(recv[rows, :], w1[:, c], preferred_element_type=jnp.float32)
            h = 0.5 * h * (1.0 + lax.erf(h * 0.7071067811865476))
            hid[:count, c] = h.astype(jnp.bfloat16)

        @pl.loop(0, 1024 // WIDE)
        def _(n):
            c = pl.ds(pl.multiple_of(n * WIDE, WIDE), WIDE)
            prod[rows, c] = jnp.dot(
                hid[:count, :], w2[:, c], preferred_element_type=jnp.float32
            ).astype(jnp.bfloat16)

        for j in range(begin, min(end, PACK - 1)):
            back[j].start()
    ret[(PACK - 1) * CAP :, :] = prod[(PACK - 1) * CAP :, :]

    gate = jnp.concatenate([gate_cols[...]] * (1024 // LANES), axis=1)
    for j in range(HALF):
        back[j].wait_recv()
    stream[...] += gate * jnp.dot(place_t[:, :ROWS], ret[:ROWS, :], preferred_element_type=jnp.float32)
    for j in range(HALF, PACK - 1):
        back[j].wait_recv()
    second = jnp.dot(place_t[:, ROWS:], ret[ROWS:, :], preferred_element_type=jnp.float32)
    out_ref[...] = (stream[...] + gate * second).astype(out_ref.dtype)

    for copy in seg_out + seg_on + sib_out:
        copy.wait_send()

    @pl.loop(0, KEPT)
    def _(p):
        for copy in plain(p):
            copy.wait_send()

    @pl.loop(0, 2 * KEPT)
    def _(n):
        picked(n).wait_send()

    @pl.loop(0, 2 * PAIRS)
    def _(n):
        forward(n).wait_send()

    for n in range(PAIRS - KEPT):
        helping(n).wait_send()
    for copy in go + back:
        copy.wait_send()


def on_device(
    queries, keys, values, residual, segments, out_weight, norm_gain, routes, gate_prob,
    expert_in, expert_out,
):
    bf16, f32 = jnp.bfloat16, jnp.float32
    hbm = pl.BlockSpec(memory_space=pl.ANY)
    vmem = pl.BlockSpec(memory_space=pltpu.VMEM)
    row = lambda vector: vector.reshape(1, -1)
    dma = pltpu.SemaphoreType.DMA
    return pl.pallas_call(
        kernel,
        out_shape=jax.ShapeDtypeStruct((ROWS, 1024), bf16),
        in_specs=[hbm] * 4 + [vmem] * 4 + [hbm] * 3,
        out_specs=vmem,
        scratch_shapes=[
            pltpu.VMEM((ROWS, 1024), bf16),
            pltpu.VMEM((2, ROWS, 1024), bf16),
            pltpu.VMEM((2, ROWS, 1024), bf16),
            pltpu.VMEM((4 * KEPT, ROWS, LANES), bf16),
            pltpu.VMEM((2 * PAIRS, ROWS, LANES), bf16),
            pltpu.VMEM((2 * KEPT, ROWS, LANES), bf16),
            pltpu.VMEM((PAIRS - KEPT, ROWS, LANES), bf16),
            pltpu.VMEM((PAIRS - KEPT, ROWS, LANES), bf16),
            pltpu.VMEM((5, 8, ROWS), jnp.int32),
            pltpu.VMEM((2, ROWS, LANES), bf16),
            pltpu.VMEM((5, ROWS, LANES), bf16),
            pltpu.VMEM((ROWS, LANES), f32),
            pltpu.VMEM((ROWS, 1024), bf16),
            pltpu.VMEM((ROWS, 1024), bf16),
            pltpu.VMEM((1024, 1024), bf16),
            pltpu.VMEM((1024, 2048), bf16),
            pltpu.VMEM((2048, 1024), bf16),
            pltpu.VMEM((ROWS, 1024), f32),
            pltpu.VMEM((PACK * CAP, ROWS), bf16),
            pltpu.VMEM((ROWS, PACK * CAP), bf16),
            pltpu.VMEM((ROWS, LANES), f32),
            pltpu.VMEM((PACK * CAP, 1024), bf16),
            pltpu.VMEM((PACK * CAP, 1024), bf16),
            pltpu.VMEM((ROWS, 2048), bf16),
            pltpu.VMEM((PACK * CAP, 1024), bf16),
            pltpu.VMEM((PACK * CAP, 1024), bf16),
            dma((7,)),
            dma((4,)),
            dma((4,)),
            dma((2, 2)),
            dma((2, 2)),
            dma((4 * KEPT,)),
            dma((4 * KEPT,)),
            dma((2 * PAIRS,)),
            dma((2 * PAIRS,)),
            dma((PAIRS - KEPT,)),
            dma((PAIRS - KEPT,)),
            dma((PACK,)),
            dma((PACK,)),
            dma((PACK,)),
            dma((PACK,)),
        ],
        compiler_params=pltpu.CompilerParams(
            collective_id=0, has_side_effects=True, vmem_limit_bytes=56 << 20
        ),
        name="layer",
    )(
        queries, keys, values, residual,
        row(segments), row(routes), row(gate_prob), row(norm_gain),
        out_weight, expert_in, expert_out,
    )


def solution(mesh):
    placed = (
        P(("dp", "pack"), None),
        P(("dp", "pack"), None),
        P(("dp", "pack"), None),
        P(("dp", "pack"), None),
        P(("dp", "pack")),
        P(),
        P(),
        P(("dp", "pack"), None),
        P(("dp", "pack")),
        P("pack", None, None),
        P("pack", None, None),
    )
    return jax.shard_map(
        on_device, mesh=mesh, in_specs=placed, out_specs=P(("dp", "pack"), None), check_vma=False
    )
```

```python
import jax
import jax.numpy as jnp
from jax import lax
from jax.experimental import pallas as pl
from jax.experimental.pallas import tpu as pltpu
from jax.sharding import PartitionSpec as P

HEADS = 16
PACK = 32
SIDE = 4
ROWS = 256
CAP = 16
PAIRS = HEADS // 2
LANES = 128
FAR_AWAY = -1e30
MESH = pl.DeviceIdType.MESH
OWN, SIB, NEAR, FAR, FWD = range(5)
KEPT = 5
WAVES = (0, 8, 20, 32)
WIDE = 1024
AHEAD = 1
PICK_ORDER = (0, 1, 6, 2, 3, 7, 4, 5, 8, 9)
UNITS = (
    ("help", 5), ("home", 5), ("home", 0), ("help", 6), ("home", 6), ("home", 1),
    ("help", 7), ("home", 7), ("home", 2), ("home", 3), ("home", 4),
)


def hops(step):
    return min(step[0], SIDE - step[0]) + min(step[1], SIDE - step[1])


STEPS = sorted(
    [(dy, dx, dc) for dy in range(SIDE) for dx in range(SIDE) for dc in (1, 0)],
    key=lambda step: (-hops(step), step[0], step[1], -step[2]),
)
HALF = PACK // 2


def moved(me, step, sign):
    y, x, core = me // (2 * SIDE), (me // 2) % SIDE, me % 2
    y = lax.rem(y + sign * step[0] + SIDE, SIDE)
    x = lax.rem(x + sign * step[1] + SIDE, SIDE)
    core = lax.rem(core + step[2], 2)
    return (y * SIDE + x) * 2 + core


def kernel(
    q_hbm, k_hbm, v_hbm, res_hbm, seg_ref, route_ref, gate_ref, gain_ref, wo_hbm, w1_hbm, w2_hbm,
    out_ref,
    qs, kt, vt, near, fwd, pick, help_out, help_in, held_a, held_b, tops_a, tops_b,
    segs, qaug, kaug, helped, att,
    res, wo, w1, w2, stream, place, place_t, gate_cols, outg, recv, hid, prod, ret,
    load_sem, seg_send, seg_recv, sib_send, sib_recv, near_send, near_recv, fwd_send, fwd_recv,
    help_send, help_recv, go_send, go_recv, back_send, back_recv,
):
    me = lax.axis_index("pack")
    core = lax.rem(me, 2)
    sibling = me + 1 - 2 * core
    across = lax.rem(me + 2 * core + PACK - 1, PACK)

    barrier = pltpu.get_barrier_semaphore()

    @pl.loop(1, PACK)
    def _(d):
        pl.semaphore_signal(
            barrier, inc=1, device_id={"pack": lax.rem(me + d, PACK)}, device_id_type=MESH
        )

    loads = [
        pltpu.make_async_copy(src, dst, load_sem.at[i])
        for i, (src, dst) in enumerate(
            [
                (k_hbm, kt.at[OWN]),
                (v_hbm, vt.at[OWN]),
                (q_hbm, qs),
                (res_hbm, res),
                (wo_hbm, wo),
                (w1_hbm.at[0], w1),
                (w2_hbm.at[0], w2),
            ]
        )
    ]
    for load in loads[:4]:
        load.start()
    segs[OWN] = jnp.broadcast_to(seg_ref[0:1, :], (8, ROWS))
    pl.semaphore_wait(barrier, PACK - 1)

    def cols(p):
        return pl.ds(pl.multiple_of(p * LANES, LANES), LANES)

    def remote(src, dst, send, recv_s, peer):
        return pltpu.make_async_remote_copy(
            src_ref=src, dst_ref=dst, send_sem=send, recv_sem=recv_s,
            device_id={"pack": peer}, device_id_type=MESH,
        )

    def plain(p):
        return [
            remote(hbm.at[:, cols(p)], near.at[2 * p + i], near_send.at[2 * p + i], near_recv.at[2 * p + i], across)
            for i, hbm in enumerate((k_hbm, v_hbm))
        ]

    def picked(n):
        at = 2 * KEPT + n
        return remote(pick.at[n], near.at[at], near_send.at[at], near_recv.at[at], across)

    def forward(n):
        return remote(near.at[n], fwd.at[n], fwd_send.at[n], fwd_recv.at[n], sibling)

    def helping(n):
        return remote(help_out.at[n], help_in.at[n], help_send.at[n], help_recv.at[n], across)

    seg_out = [
        remote(segs.at[OWN], segs.at[NEAR], seg_send.at[0], seg_recv.at[0], across),
        remote(segs.at[OWN], segs.at[SIB], seg_send.at[1], seg_recv.at[1], sibling),
    ]
    seg_on = [
        remote(segs.at[SIB], segs.at[FAR], seg_send.at[2], seg_recv.at[2], across),
        remote(segs.at[NEAR], segs.at[FWD], seg_send.at[3], seg_recv.at[3], sibling),
    ]
    first, rest = pl.ds(0, KEPT * LANES), pl.ds(KEPT * LANES, (PAIRS - KEPT) * LANES)
    sib_out = [
        remote(hbm.at[:, c], tile.at[SIB, :, c], sib_send.at[i, n], sib_recv.at[i, n], sibling)
        for n, c in enumerate((first, rest))
        for i, (hbm, tile) in enumerate(((k_hbm, kt), (v_hbm, vt)))
    ]
    for copy in seg_out + plain(0) + sib_out + plain(1):
        copy.start()

    def edge(row, at_end):
        return jnp.where(at_end, row[:, ROWS - 1 :], row[:, :1])

    for copy in seg_out:
        copy.wait_recv()
    for copy in seg_on:
        copy.start()
    for load in loads[:4]:
        load.wait()
    for copy in sib_out[:2]:
        copy.wait_recv()
    last = core == 1
    sib_edge = edge(segs[SIB, 0:1, :], last)
    near_edge = edge(segs[NEAR, 0:1, :], core == 0)
    own_edge = edge(segs[OWN, 0:1, :], last)
    wide_here = jnp.broadcast_to(sib_edge, (ROWS, LANES)) == jnp.broadcast_to(near_edge, (ROWS, LANES))
    usual = [(t.at[OWN], p) for p in range(KEPT, PAIRS) for t in (kt, vt)]
    usual += [(qs, p) for p in range(KEPT, PAIRS)]
    for n in range(2 * KEPT):
        wide = (kt, vt)[n % 2][SIB, :, LANES * (n // 2) : LANES * (n // 2 + 1)]
        if n < len(usual):
            src, p = usual[n]
            wide = jnp.where(wide_here, wide, src[:, LANES * p : LANES * (p + 1)])
        pick[n] = wide

    for n in PICK_ORDER:
        picked(n).start()

    @pl.loop(2, KEPT)
    def _(p):
        for copy in plain(p):
            copy.start()

    for load in loads[4:]:
        load.start()

    def image_rows(seg):
        spread = jnp.broadcast_to(seg[0:1, :], (LANES, ROWS))
        return spread == lax.broadcasted_iota(jnp.int32, (LANES, ROWS), 0)

    def query_marks(rows):
        return jnp.where(rows, FAR_AWAY, 0.0).T.astype(jnp.bfloat16)

    def key_marks(rows):
        return jnp.where(rows, 0.0, 1.0).T.astype(jnp.bfloat16)

    own_rows, near_rows = image_rows(segs[OWN]), image_rows(segs[NEAR])
    qaug[0] = query_marks(own_rows)
    qaug[1] = query_marks(near_rows)
    kaug[OWN] = key_marks(own_rows)
    kaug[NEAR] = key_marks(near_rows)
    kaug[SIB] = key_marks(image_rows(segs[SIB]))
    for copy in seg_on:
        copy.wait_recv()
    kaug[FWD] = key_marks(image_rows(segs[FWD]))
    far_edge = edge(segs[FAR, 0:1, :], core == 0)
    wide_there = jnp.broadcast_to(far_edge, (LANES, ROWS)) == jnp.broadcast_to(own_edge, (LANES, ROWS))
    kaug[FAR] = key_marks(jnp.logical_and(wide_there, image_rows(segs[FAR])))
    in_crossing = jnp.broadcast_to(segs[OWN, 0:1, :], (LANES, ROWS)) == jnp.broadcast_to(own_edge, (LANES, ROWS))
    helped[...] = jnp.where(jnp.logical_and(wide_there, in_crossing), 1.0, 0.0).T

    expert_of = jnp.zeros((PACK, ROWS), jnp.int32)
    place_iota = lax.broadcasted_iota(jnp.int32, (PACK, ROWS), 0)
    for j, step in enumerate(STEPS):
        expert_of = jnp.where(place_iota == j, moved(me, step, 1), expert_of)
    chosen = jnp.broadcast_to(route_ref[0:1, :], (PACK, ROWS)) == expert_of
    earlier = lax.broadcasted_iota(jnp.int32, (ROWS, ROWS), 0) < lax.broadcasted_iota(
        jnp.int32, (ROWS, ROWS), 1
    )
    rank = jnp.dot(
        jnp.where(chosen, 1.0, 0.0).astype(jnp.bfloat16),
        jnp.where(earlier, 1.0, 0.0).astype(jnp.bfloat16),
        preferred_element_type=jnp.float32,
    )
    slot = jnp.where(chosen, rank, -1.0)
    slot_iota = lax.broadcasted_iota(jnp.int32, (CAP, ROWS), 0).astype(jnp.float32)
    for j in range(PACK):
        hit = jnp.broadcast_to(slot[j : j + 1, :], (CAP, ROWS)) == slot_iota
        hit = jnp.where(hit, 1.0, 0.0)
        place[CAP * j : CAP * (j + 1), :] = hit.astype(jnp.bfloat16)
    for j in range(0, PACK * CAP, LANES):
        place_t[:, j : j + LANES] = place[j : j + LANES, :].astype(jnp.float32).T.astype(jnp.bfloat16)
    gate_cols[...] = jnp.broadcast_to(gate_ref[0:1, :], (LANES, ROWS)).T
    stream[...] = res[...].astype(jnp.float32)

    exp_scale = float((1024 // HEADS) ** -0.5 * 1.4426950408889634)
    low_lanes = lax.broadcasted_iota(jnp.int32, (ROWS, LANES), 1) < LANES // 2
    ones = jnp.ones((ROWS, LANES), jnp.bfloat16)

    def at_home(p, place_of):
        c = slice(p * LANES, (p + 1) * LANES)
        return (lambda: kt[place_of, :, c], lambda: kaug[place_of], lambda: vt[place_of, :, c])

    def arrived(buf, at, place_of):
        return (lambda: buf[at], lambda: kaug[place_of], lambda: buf[at + 1])

    def tiles_of(kind, p):
        tiles = [at_home(p, OWN), at_home(p, SIB), arrived(near, 2 * p, NEAR)]
        if kind == "home":
            tiles.append(arrived(fwd, 2 * p, FWD))
            if p < KEPT:
                tiles.append(arrived(near, 2 * KEPT + 2 * p, FAR))
        return tiles

    def begin_unit(kind, p, held, tops):
        if kind == "home":
            both, marks = qs[:, p * LANES : (p + 1) * LANES], qaug[0]
        else:
            both, marks = near[2 * PAIRS + p - KEPT], qaug[1]
        zero = jnp.zeros_like(both)
        lhs = jnp.concatenate(
            [
                jnp.concatenate([jnp.where(low_lanes, both, zero), marks], axis=1),
                jnp.concatenate([jnp.where(low_lanes, zero, both), marks], axis=1),
            ],
            axis=0,
        )
        top = None
        for n, (key, mark, _) in enumerate(tiles_of(kind, p)):
            scores = lax.dot_general(
                lhs,
                jnp.concatenate([key(), mark()], axis=1),
                (((1,), (1,)), ((), ())),
                preferred_element_type=jnp.float32,
            )
            held[n] = scores
            top = scores if top is None else jnp.maximum(top, scores)
        tops[...] = jnp.broadcast_to(jnp.max(top, axis=1, keepdims=True), (2 * ROWS, LANES))

    def finish_unit(kind, p, held, tops):
        top = jnp.concatenate([tops[...], tops[...]], axis=1)
        summed = jnp.zeros((2 * ROWS, 2 * LANES), jnp.float32)
        for n, (_, _, value) in enumerate(tiles_of(kind, p)):
            weights = jnp.exp2((held[n] - top) * exp_scale).astype(jnp.bfloat16)
            rhs = jnp.concatenate([value(), ones], axis=1)
            summed = summed + jnp.dot(weights, rhs, preferred_element_type=jnp.float32)
        both = summed[:, :LANES] / summed[:, LANES:]
        attended = jnp.where(low_lanes, both[:ROWS], both[ROWS:]).astype(jnp.bfloat16)
        if kind == "help":
            help_out[p - KEPT] = attended
            helping(p - KEPT).start()
        elif p >= KEPT:
            att[:, p * LANES : (p + 1) * LANES] = attended
        else:
            stream[...] += jnp.dot(
                attended, wo[p * LANES : (p + 1) * LANES, :], preferred_element_type=jnp.float32
            )

    came = set()

    def near_came(at):
        if at not in came:
            came.add(at)
            copy = plain(at // 2)[at % 2] if at < 2 * KEPT else picked(at - 2 * KEPT)
            copy.wait_recv()
            if at < 2 * PAIRS:
                forward(at).start()

    def unit_came(kind, p):
        near_came(2 * p)
        near_came(2 * p + 1)
        if kind == "help":
            near_came(2 * PAIRS + p - KEPT)
        elif p < KEPT:
            near_came(2 * KEPT + 2 * p)
            near_came(2 * KEPT + 2 * p + 1)

    for at in range(4):
        near_came(at)
    for copy in sib_out[2:]:
        copy.wait_recv()
    loads[4].wait()
    stages = ((held_a, tops_a), (held_b, tops_b))
    for n, unit in enumerate(UNITS):
        for later in UNITS[n : n + 1 + AHEAD]:
            unit_came(*later)
        if unit[0] == "home":
            forward(2 * unit[1]).wait_recv()
            forward(2 * unit[1] + 1).wait_recv()
        begin_unit(*unit, *stages[n % 2])
        if n:
            finish_unit(*UNITS[n - 1], *stages[(n - 1) % 2])
    finish_unit(*UNITS[-1], *stages[(len(UNITS) - 1) % 2])

    for n in range(PAIRS - KEPT):
        helping(n).wait_recv()
        c = slice((KEPT + n) * LANES, (KEPT + n + 1) * LANES)
        att[:, c] = jnp.where(helped[...] > 0.5, help_in[n], att[:, c])

    x = stream[...] + jnp.dot(
        att[:, KEPT * LANES :], wo[KEPT * LANES :, :], preferred_element_type=jnp.float32
    )
    stream[...] = x
    mean = jnp.mean(x, axis=1, keepdims=True)
    centered = x - mean
    var = jnp.mean(centered * centered, axis=1, keepdims=True)
    normed = (centered * lax.rsqrt(var + 1e-6) * gain_ref[0:1, :]).astype(jnp.bfloat16)

    def block(j):
        return pl.ds(j * CAP, CAP)

    go = [
        remote(outg.at[block(j)], recv.at[block(j)], go_send.at[j], go_recv.at[j], moved(me, step, 1))
        for j, step in enumerate(STEPS[:-1])
    ]
    back = [
        remote(prod.at[block(j)], ret.at[block(j)], back_send.at[j], back_recv.at[j], moved(me, step, -1))
        for j, step in enumerate(STEPS[:-1])
    ]
    part = 128
    for start in range(0, PACK * CAP, part):
        outg[start : start + part, :] = jnp.dot(
            place[start : start + part, :], normed, preferred_element_type=jnp.float32
        ).astype(jnp.bfloat16)
        for j in range(start // CAP, min((start + part) // CAP, PACK - 1)):
            go[j].start()
    recv[(PACK - 1) * CAP :, :] = outg[(PACK - 1) * CAP :, :]

    loads[5].wait()
    loads[6].wait()

    for begin, end in zip(WAVES, WAVES[1:]):
        rows, count = pl.ds(begin * CAP, (end - begin) * CAP), (end - begin) * CAP
        for j in range(begin, min(end, PACK - 1)):
            go[j].wait_recv()

        @pl.loop(0, 2048 // WIDE)
        def _(n):
            c = pl.ds(pl.multiple_of(n * WIDE, WIDE), WIDE)
            h = jnp.dot(recv[rows, :], w1[:, c], preferred_element_type=jnp.float32)
            h = 0.5 * h * (1.0 + lax.erf(h * 0.7071067811865476))
            hid[:count, c] = h.astype(jnp.bfloat16)

        @pl.loop(0, 1024 // WIDE)
        def _(n):
            c = pl.ds(pl.multiple_of(n * WIDE, WIDE), WIDE)
            prod[rows, c] = jnp.dot(
                hid[:count, :], w2[:, c], preferred_element_type=jnp.float32
            ).astype(jnp.bfloat16)

        for j in range(begin, min(end, PACK - 1)):
            back[j].start()
    ret[(PACK - 1) * CAP :, :] = prod[(PACK - 1) * CAP :, :]

    gate = jnp.concatenate([gate_cols[...]] * (1024 // LANES), axis=1)
    for j in range(HALF):
        back[j].wait_recv()
    stream[...] += gate * jnp.dot(place_t[:, :ROWS], ret[:ROWS, :], preferred_element_type=jnp.float32)
    for j in range(HALF, PACK - 1):
        back[j].wait_recv()
    second = jnp.dot(place_t[:, ROWS:], ret[ROWS:, :], preferred_element_type=jnp.float32)
    out_ref[...] = (stream[...] + gate * second).astype(out_ref.dtype)

    for copy in seg_out + seg_on + sib_out:
        copy.wait_send()

    @pl.loop(0, KEPT)
    def _(p):
        for copy in plain(p):
            copy.wait_send()

    @pl.loop(0, 2 * KEPT)
    def _(n):
        picked(n).wait_send()

    @pl.loop(0, 2 * PAIRS)
    def _(n):
        forward(n).wait_send()

    for n in range(PAIRS - KEPT):
        helping(n).wait_send()
    for copy in go + back:
        copy.wait_send()


def on_device(
    queries, keys, values, residual, segments, out_weight, norm_gain, routes, gate_prob,
    expert_in, expert_out,
):
    bf16, f32 = jnp.bfloat16, jnp.float32
    hbm = pl.BlockSpec(memory_space=pl.ANY)
    vmem = pl.BlockSpec(memory_space=pltpu.VMEM)
    row = lambda vector: vector.reshape(1, -1)
    dma = pltpu.SemaphoreType.DMA
    return pl.pallas_call(
        kernel,
        out_shape=jax.ShapeDtypeStruct((ROWS, 1024), bf16),
        in_specs=[hbm] * 4 + [vmem] * 4 + [hbm] * 3,
        out_specs=vmem,
        scratch_shapes=[
            pltpu.VMEM((ROWS, 1024), bf16),
            pltpu.VMEM((2, ROWS, 1024), bf16),
            pltpu.VMEM((2, ROWS, 1024), bf16),
            pltpu.VMEM((4 * KEPT, ROWS, LANES), bf16),
            pltpu.VMEM((2 * PAIRS, ROWS, LANES), bf16),
            pltpu.VMEM((2 * KEPT, ROWS, LANES), bf16),
            pltpu.VMEM((PAIRS - KEPT, ROWS, LANES), bf16),
            pltpu.VMEM((PAIRS - KEPT, ROWS, LANES), bf16),
            pltpu.VMEM((5, 2 * ROWS, ROWS), f32),
            pltpu.VMEM((5, 2 * ROWS, ROWS), f32),
            pltpu.VMEM((2 * ROWS, LANES), f32),
            pltpu.VMEM((2 * ROWS, LANES), f32),
            pltpu.VMEM((5, 8, ROWS), jnp.int32),
            pltpu.VMEM((2, ROWS, LANES), bf16),
            pltpu.VMEM((5, ROWS, LANES), bf16),
            pltpu.VMEM((ROWS, LANES), f32),
            pltpu.VMEM((ROWS, 1024), bf16),
            pltpu.VMEM((ROWS, 1024), bf16),
            pltpu.VMEM((1024, 1024), bf16),
            pltpu.VMEM((1024, 2048), bf16),
            pltpu.VMEM((2048, 1024), bf16),
            pltpu.VMEM((ROWS, 1024), f32),
            pltpu.VMEM((PACK * CAP, ROWS), bf16),
            pltpu.VMEM((ROWS, PACK * CAP), bf16),
            pltpu.VMEM((ROWS, LANES), f32),
            pltpu.VMEM((PACK * CAP, 1024), bf16),
            pltpu.VMEM((PACK * CAP, 1024), bf16),
            pltpu.VMEM((ROWS, 2048), bf16),
            pltpu.VMEM((PACK * CAP, 1024), bf16),
            pltpu.VMEM((PACK * CAP, 1024), bf16),
            dma((7,)),
            dma((4,)),
            dma((4,)),
            dma((2, 2)),
            dma((2, 2)),
            dma((4 * KEPT,)),
            dma((4 * KEPT,)),
            dma((2 * PAIRS,)),
            dma((2 * PAIRS,)),
            dma((PAIRS - KEPT,)),
            dma((PAIRS - KEPT,)),
            dma((PACK,)),
            dma((PACK,)),
            dma((PACK,)),
            dma((PACK,)),
        ],
        compiler_params=pltpu.CompilerParams(
            collective_id=0, has_side_effects=True, vmem_limit_bytes=56 << 20
        ),
        name="layer",
    )(
        queries, keys, values, residual,
        row(segments), row(routes), row(gate_prob), row(norm_gain),
        out_weight, expert_in, expert_out,
    )


def solution(mesh):
    placed = (
        P(("dp", "pack"), None),
        P(("dp", "pack"), None),
        P(("dp", "pack"), None),
        P(("dp", "pack"), None),
        P(("dp", "pack")),
        P(),
        P(),
        P(("dp", "pack"), None),
        P(("dp", "pack")),
        P("pack", None, None),
        P("pack", None, None),
    )
    return jax.shard_map(
        on_device, mesh=mesh, in_specs=placed, out_specs=P(("dp", "pack"), None), check_vma=False
    )
```

```python
import jax
import jax.numpy as jnp
from jax import lax
from jax.experimental import pallas as pl
from jax.experimental.pallas import tpu as pltpu
from jax.sharding import PartitionSpec as P

HEADS = 16
PACK = 32
SIDE = 4
ROWS = 256
CAP = 16
PAIRS = HEADS // 2
LANES = 128
FAR_AWAY = -1e30
MESH = pl.DeviceIdType.MESH
OWN, SIB, NEAR, FAR, FWD = range(5)
KEPT = 5
WAVES = (0, 8, 20, 32)
WIDE = 1024
AHEAD = 1
PICK_ORDER = (0, 1, 6, 2, 3, 7, 4, 5, 8, 9)
UNITS = tuple(("part", pair) for pair in range(PAIRS)) + (
    ("help", 5), ("home", 5), ("home", 0), ("help", 6), ("home", 6), ("home", 1),
    ("help", 7), ("home", 7), ("home", 2), ("home", 3), ("home", 4),
)


def hops(step):
    return min(step[0], SIDE - step[0]) + min(step[1], SIDE - step[1])


STEPS = sorted(
    [(dy, dx, dc) for dy in range(SIDE) for dx in range(SIDE) for dc in (1, 0)],
    key=lambda step: (-hops(step), step[0], step[1], -step[2]),
)
HALF = PACK // 2


def moved(me, step, sign):
    y, x, core = me // (2 * SIDE), (me // 2) % SIDE, me % 2
    y = lax.rem(y + sign * step[0] + SIDE, SIDE)
    x = lax.rem(x + sign * step[1] + SIDE, SIDE)
    core = lax.rem(core + step[2], 2)
    return (y * SIDE + x) * 2 + core


def kernel(
    q_hbm, k_hbm, v_hbm, res_hbm, seg_ref, route_ref, gate_ref, gain_ref, wo_hbm, w1_hbm, w2_hbm,
    out_ref,
    qs, kt, vt, near, fwd, pick, help_out, help_in, held_a, held_b, tops_a, tops_b, parts, part_tops,
    segs, qaug, kaug, helped, att,
    res, wo, w1, w2, stream, place, place_t, gate_cols, outg, recv, hid, prod, ret,
    load_sem, seg_send, seg_recv, sib_send, sib_recv, near_send, near_recv, fwd_send, fwd_recv,
    help_send, help_recv, go_send, go_recv, back_send, back_recv,
):
    me = lax.axis_index("pack")
    core = lax.rem(me, 2)
    sibling = me + 1 - 2 * core
    across = lax.rem(me + 2 * core + PACK - 1, PACK)

    barrier = pltpu.get_barrier_semaphore()

    @pl.loop(1, PACK)
    def _(d):
        pl.semaphore_signal(
            barrier, inc=1, device_id={"pack": lax.rem(me + d, PACK)}, device_id_type=MESH
        )

    loads = [
        pltpu.make_async_copy(src, dst, load_sem.at[i])
        for i, (src, dst) in enumerate(
            [
                (k_hbm, kt.at[OWN]),
                (v_hbm, vt.at[OWN]),
                (q_hbm, qs),
                (res_hbm, res),
                (wo_hbm, wo),
                (w1_hbm.at[0], w1),
                (w2_hbm.at[0], w2),
            ]
        )
    ]
    for load in loads[:4]:
        load.start()
    segs[OWN] = jnp.broadcast_to(seg_ref[0:1, :], (8, ROWS))
    pl.semaphore_wait(barrier, PACK - 1)

    def cols(p):
        return pl.ds(pl.multiple_of(p * LANES, LANES), LANES)

    def remote(src, dst, send, recv_s, peer):
        return pltpu.make_async_remote_copy(
            src_ref=src, dst_ref=dst, send_sem=send, recv_sem=recv_s,
            device_id={"pack": peer}, device_id_type=MESH,
        )

    def plain(p):
        return [
            remote(hbm.at[:, cols(p)], near.at[2 * p + i], near_send.at[2 * p + i], near_recv.at[2 * p + i], across)
            for i, hbm in enumerate((k_hbm, v_hbm))
        ]

    def picked(n):
        at = 2 * KEPT + n
        return remote(pick.at[n], near.at[at], near_send.at[at], near_recv.at[at], across)

    def forward(n):
        return remote(near.at[n], fwd.at[n], fwd_send.at[n], fwd_recv.at[n], sibling)

    def helping(n):
        return remote(help_out.at[n], help_in.at[n], help_send.at[n], help_recv.at[n], across)

    seg_out = [
        remote(segs.at[OWN], segs.at[NEAR], seg_send.at[0], seg_recv.at[0], across),
        remote(segs.at[OWN], segs.at[SIB], seg_send.at[1], seg_recv.at[1], sibling),
    ]
    seg_on = [
        remote(segs.at[SIB], segs.at[FAR], seg_send.at[2], seg_recv.at[2], across),
        remote(segs.at[NEAR], segs.at[FWD], seg_send.at[3], seg_recv.at[3], sibling),
    ]
    first, rest = pl.ds(0, KEPT * LANES), pl.ds(KEPT * LANES, (PAIRS - KEPT) * LANES)
    sib_out = [
        remote(hbm.at[:, c], tile.at[SIB, :, c], sib_send.at[i, n], sib_recv.at[i, n], sibling)
        for n, c in enumerate((first, rest))
        for i, (hbm, tile) in enumerate(((k_hbm, kt), (v_hbm, vt)))
    ]
    for copy in seg_out + plain(0) + sib_out + plain(1):
        copy.start()

    expert_of = jnp.zeros((PACK, ROWS), jnp.int32)
    place_iota = lax.broadcasted_iota(jnp.int32, (PACK, ROWS), 0)
    for j, step in enumerate(STEPS):
        expert_of = jnp.where(place_iota == j, moved(me, step, 1), expert_of)
    chosen = jnp.broadcast_to(route_ref[0:1, :], (PACK, ROWS)) == expert_of
    earlier = lax.broadcasted_iota(jnp.int32, (ROWS, ROWS), 0) < lax.broadcasted_iota(
        jnp.int32, (ROWS, ROWS), 1
    )
    rank = jnp.dot(
        jnp.where(chosen, 1.0, 0.0).astype(jnp.bfloat16),
        jnp.where(earlier, 1.0, 0.0).astype(jnp.bfloat16),
        preferred_element_type=jnp.float32,
    )
    slot = jnp.where(chosen, rank, -1.0)
    slot_iota = lax.broadcasted_iota(jnp.int32, (CAP, ROWS), 0).astype(jnp.float32)
    for j in range(PACK):
        hit = jnp.broadcast_to(slot[j : j + 1, :], (CAP, ROWS)) == slot_iota
        hit = jnp.where(hit, 1.0, 0.0)
        place[CAP * j : CAP * (j + 1), :] = hit.astype(jnp.bfloat16)
    for j in range(0, PACK * CAP, LANES):
        place_t[:, j : j + LANES] = place[j : j + LANES, :].astype(jnp.float32).T.astype(jnp.bfloat16)
    gate_cols[...] = jnp.broadcast_to(gate_ref[0:1, :], (LANES, ROWS)).T

    def edge(row, at_end):
        return jnp.where(at_end, row[:, ROWS - 1 :], row[:, :1])

    for copy in seg_out:
        copy.wait_recv()
    for copy in seg_on:
        copy.start()
    for load in loads[:4]:
        load.wait()
    for copy in sib_out[:2]:
        copy.wait_recv()
    last = core == 1
    sib_edge = edge(segs[SIB, 0:1, :], last)
    near_edge = edge(segs[NEAR, 0:1, :], core == 0)
    own_edge = edge(segs[OWN, 0:1, :], last)
    wide_here = jnp.broadcast_to(sib_edge, (ROWS, LANES)) == jnp.broadcast_to(near_edge, (ROWS, LANES))
    usual = [(t.at[OWN], p) for p in range(KEPT, PAIRS) for t in (kt, vt)]
    usual += [(qs, p) for p in range(KEPT, PAIRS)]
    for n in range(2 * KEPT):
        wide = (kt, vt)[n % 2][SIB, :, LANES * (n // 2) : LANES * (n // 2 + 1)]
        if n < len(usual):
            src, p = usual[n]
            wide = jnp.where(wide_here, wide, src[:, LANES * p : LANES * (p + 1)])
        pick[n] = wide

    for n in PICK_ORDER:
        picked(n).start()

    @pl.loop(2, KEPT)
    def _(p):
        for copy in plain(p):
            copy.start()

    for load in loads[4:]:
        load.start()

    def image_rows(seg):
        spread = jnp.broadcast_to(seg[0:1, :], (LANES, ROWS))
        return spread == lax.broadcasted_iota(jnp.int32, (LANES, ROWS), 0)

    def query_marks(rows):
        return jnp.where(rows, FAR_AWAY, 0.0).T.astype(jnp.bfloat16)

    def key_marks(rows):
        return jnp.where(rows, 0.0, 1.0).T.astype(jnp.bfloat16)

    own_rows, near_rows = image_rows(segs[OWN]), image_rows(segs[NEAR])
    qaug[0] = query_marks(own_rows)
    qaug[1] = query_marks(near_rows)
    kaug[OWN] = key_marks(own_rows)
    kaug[NEAR] = key_marks(near_rows)
    kaug[SIB] = key_marks(image_rows(segs[SIB]))
    exp_scale = float((1024 // HEADS) ** -0.5 * 1.4426950408889634)
    low_lanes = lax.broadcasted_iota(jnp.int32, (ROWS, LANES), 1) < LANES // 2
    ones = jnp.ones((ROWS, LANES), jnp.bfloat16)

    def at_home(p, place_of):
        c = slice(p * LANES, (p + 1) * LANES)
        return (lambda: kt[place_of, :, c], lambda: kaug[place_of], lambda: vt[place_of, :, c])

    def arrived(buf, at, place_of):
        return (lambda: buf[at], lambda: kaug[place_of], lambda: buf[at + 1])

    def tiles_of(kind, p):
        here = [at_home(p, OWN), at_home(p, SIB)]
        if kind == "part":
            return here
        tiles = [arrived(near, 2 * p, NEAR)]
        if kind == "help":
            return here + tiles
        tiles.append(arrived(fwd, 2 * p, FWD))
        if p < KEPT:
            tiles.append(arrived(near, 2 * KEPT + 2 * p, FAR))
        return tiles

    def begin_unit(kind, p, held, tops):
        if kind != "help":
            both, marks = qs[:, p * LANES : (p + 1) * LANES], qaug[0]
        else:
            both, marks = near[2 * PAIRS + p - KEPT], qaug[1]
        zero = jnp.zeros_like(both)
        lhs = jnp.concatenate(
            [
                jnp.concatenate([jnp.where(low_lanes, both, zero), marks], axis=1),
                jnp.concatenate([jnp.where(low_lanes, zero, both), marks], axis=1),
            ],
            axis=0,
        )
        top = None
        for n, (key, mark, _) in enumerate(tiles_of(kind, p)):
            scores = lax.dot_general(
                lhs,
                jnp.concatenate([key(), mark()], axis=1),
                (((1,), (1,)), ((), ())),
                preferred_element_type=jnp.float32,
            )
            held[n] = scores
            top = scores if top is None else jnp.maximum(top, scores)
        top = jnp.broadcast_to(jnp.max(top, axis=1, keepdims=True), (2 * ROWS, LANES))
        if kind == "home":
            top = jnp.maximum(top, part_tops[p])
        tops[...] = top

    def finish_unit(kind, p, held, tops):
        top = jnp.concatenate([tops[...], tops[...]], axis=1)
        summed = jnp.zeros((2 * ROWS, 2 * LANES), jnp.float32)
        if kind == "home":
            shrink = jnp.exp2((part_tops[p] - tops[...]) * exp_scale)
            summed = parts[p] * jnp.concatenate([shrink, shrink], axis=1)
        for n, (_, _, value) in enumerate(tiles_of(kind, p)):
            weights = jnp.exp2((held[n] - top) * exp_scale).astype(jnp.bfloat16)
            rhs = jnp.concatenate([value(), ones], axis=1)
            summed = summed + jnp.dot(weights, rhs, preferred_element_type=jnp.float32)
        if kind == "part":
            parts[p] = summed
            part_tops[p] = tops[...]
            return
        both = summed[:, :LANES] / summed[:, LANES:]
        attended = jnp.where(low_lanes, both[:ROWS], both[ROWS:]).astype(jnp.bfloat16)
        if kind == "help":
            help_out[p - KEPT] = attended
            helping(p - KEPT).start()
        else:
            att[:, p * LANES : (p + 1) * LANES] = attended

    came = set()

    def near_came(at):
        if at not in came:
            came.add(at)
            copy = plain(at // 2)[at % 2] if at < 2 * KEPT else picked(at - 2 * KEPT)
            copy.wait_recv()
            if at < 2 * PAIRS:
                forward(at).start()

    def unit_came(kind, p):
        if kind == "part":
            return
        near_came(2 * p)
        near_came(2 * p + 1)
        if kind == "help":
            near_came(2 * PAIRS + p - KEPT)
        elif p < KEPT:
            near_came(2 * KEPT + 2 * p)
            near_came(2 * KEPT + 2 * p + 1)

    def marks_of_two_hops():
        for copy in seg_on:
            copy.wait_recv()
        kaug[FWD] = key_marks(image_rows(segs[FWD]))
        far_edge = edge(segs[FAR, 0:1, :], core == 0)
        wide_there = jnp.broadcast_to(far_edge, (LANES, ROWS)) == jnp.broadcast_to(own_edge, (LANES, ROWS))
        kaug[FAR] = key_marks(jnp.logical_and(wide_there, image_rows(segs[FAR])))
        in_crossing = jnp.broadcast_to(segs[OWN, 0:1, :], (LANES, ROWS)) == jnp.broadcast_to(own_edge, (LANES, ROWS))
        helped[...] = jnp.where(jnp.logical_and(wide_there, in_crossing), 1.0, 0.0).T

    for copy in sib_out[2:]:
        copy.wait_recv()
    stages = ((held_a, tops_a), (held_b, tops_b))
    for n, unit in enumerate(UNITS):
        if n == 4:
            for at in range(4):
                near_came(at)
        for later in UNITS[n : n + 1 + AHEAD]:
            unit_came(*later)
        if n == PAIRS:
            marks_of_two_hops()
        if unit[0] == "home":
            forward(2 * unit[1]).wait_recv()
            forward(2 * unit[1] + 1).wait_recv()
        begin_unit(*unit, *stages[n % 2])
        if n:
            finish_unit(*UNITS[n - 1], *stages[(n - 1) % 2])
    finish_unit(*UNITS[-1], *stages[(len(UNITS) - 1) % 2])

    loads[4].wait()
    kept = KEPT * LANES
    stream[...] = res[...].astype(jnp.float32) + jnp.dot(
        att[:, :kept], wo[:kept, :], preferred_element_type=jnp.float32
    )
    for n in range(PAIRS - KEPT):
        helping(n).wait_recv()
        c = slice((KEPT + n) * LANES, (KEPT + n + 1) * LANES)
        att[:, c] = jnp.where(helped[...] > 0.5, help_in[n], att[:, c])

    x = stream[...] + jnp.dot(
        att[:, KEPT * LANES :], wo[KEPT * LANES :, :], preferred_element_type=jnp.float32
    )
    stream[...] = x
    mean = jnp.mean(x, axis=1, keepdims=True)
    centered = x - mean
    var = jnp.mean(centered * centered, axis=1, keepdims=True)
    normed = (centered * lax.rsqrt(var + 1e-6) * gain_ref[0:1, :]).astype(jnp.bfloat16)

    def block(j):
        return pl.ds(j * CAP, CAP)

    go = [
        remote(outg.at[block(j)], recv.at[block(j)], go_send.at[j], go_recv.at[j], moved(me, step, 1))
        for j, step in enumerate(STEPS[:-1])
    ]
    back = [
        remote(prod.at[block(j)], ret.at[block(j)], back_send.at[j], back_recv.at[j], moved(me, step, -1))
        for j, step in enumerate(STEPS[:-1])
    ]
    part = 128
    for start in range(0, PACK * CAP, part):
        outg[start : start + part, :] = jnp.dot(
            place[start : start + part, :], normed, preferred_element_type=jnp.float32
        ).astype(jnp.bfloat16)
        for j in range(start // CAP, min((start + part) // CAP, PACK - 1)):
            go[j].start()
    recv[(PACK - 1) * CAP :, :] = outg[(PACK - 1) * CAP :, :]

    loads[5].wait()
    loads[6].wait()

    for begin, end in zip(WAVES, WAVES[1:]):
        rows, count = pl.ds(begin * CAP, (end - begin) * CAP), (end - begin) * CAP
        for j in range(begin, min(end, PACK - 1)):
            go[j].wait_recv()

        @pl.loop(0, 2048 // WIDE)
        def _(n):
            c = pl.ds(pl.multiple_of(n * WIDE, WIDE), WIDE)
            h = jnp.dot(recv[rows, :], w1[:, c], preferred_element_type=jnp.float32)
            h = 0.5 * h * (1.0 + lax.erf(h * 0.7071067811865476))
            hid[:count, c] = h.astype(jnp.bfloat16)

        @pl.loop(0, 1024 // WIDE)
        def _(n):
            c = pl.ds(pl.multiple_of(n * WIDE, WIDE), WIDE)
            prod[rows, c] = jnp.dot(
                hid[:count, :], w2[:, c], preferred_element_type=jnp.float32
            ).astype(jnp.bfloat16)

        for j in range(begin, min(end, PACK - 1)):
            back[j].start()
    ret[(PACK - 1) * CAP :, :] = prod[(PACK - 1) * CAP :, :]

    gate = jnp.concatenate([gate_cols[...]] * (1024 // LANES), axis=1)
    for j in range(HALF):
        back[j].wait_recv()
    stream[...] += gate * jnp.dot(place_t[:, :ROWS], ret[:ROWS, :], preferred_element_type=jnp.float32)
    for j in range(HALF, PACK - 1):
        back[j].wait_recv()
    second = jnp.dot(place_t[:, ROWS:], ret[ROWS:, :], preferred_element_type=jnp.float32)
    out_ref[...] = (stream[...] + gate * second).astype(out_ref.dtype)

    for copy in seg_out + seg_on + sib_out:
        copy.wait_send()

    @pl.loop(0, KEPT)
    def _(p):
        for copy in plain(p):
            copy.wait_send()

    @pl.loop(0, 2 * KEPT)
    def _(n):
        picked(n).wait_send()

    @pl.loop(0, 2 * PAIRS)
    def _(n):
        forward(n).wait_send()

    for n in range(PAIRS - KEPT):
        helping(n).wait_send()
    for copy in go + back:
        copy.wait_send()


def on_device(
    queries, keys, values, residual, segments, out_weight, norm_gain, routes, gate_prob,
    expert_in, expert_out,
):
    bf16, f32 = jnp.bfloat16, jnp.float32
    hbm = pl.BlockSpec(memory_space=pl.ANY)
    vmem = pl.BlockSpec(memory_space=pltpu.VMEM)
    row = lambda vector: vector.reshape(1, -1)
    dma = pltpu.SemaphoreType.DMA
    return pl.pallas_call(
        kernel,
        out_shape=jax.ShapeDtypeStruct((ROWS, 1024), bf16),
        in_specs=[hbm] * 4 + [vmem] * 4 + [hbm] * 3,
        out_specs=vmem,
        scratch_shapes=[
            pltpu.VMEM((ROWS, 1024), bf16),
            pltpu.VMEM((2, ROWS, 1024), bf16),
            pltpu.VMEM((2, ROWS, 1024), bf16),
            pltpu.VMEM((4 * KEPT, ROWS, LANES), bf16),
            pltpu.VMEM((2 * PAIRS, ROWS, LANES), bf16),
            pltpu.VMEM((2 * KEPT, ROWS, LANES), bf16),
            pltpu.VMEM((PAIRS - KEPT, ROWS, LANES), bf16),
            pltpu.VMEM((PAIRS - KEPT, ROWS, LANES), bf16),
            pltpu.VMEM((3, 2 * ROWS, ROWS), f32),
            pltpu.VMEM((3, 2 * ROWS, ROWS), f32),
            pltpu.VMEM((2 * ROWS, LANES), f32),
            pltpu.VMEM((2 * ROWS, LANES), f32),
            pltpu.VMEM((PAIRS, 2 * ROWS, 2 * LANES), f32),
            pltpu.VMEM((PAIRS, 2 * ROWS, LANES), f32),
            pltpu.VMEM((5, 8, ROWS), jnp.int32),
            pltpu.VMEM((2, ROWS, LANES), bf16),
            pltpu.VMEM((5, ROWS, LANES), bf16),
            pltpu.VMEM((ROWS, LANES), f32),
            pltpu.VMEM((ROWS, 1024), bf16),
            pltpu.VMEM((ROWS, 1024), bf16),
            pltpu.VMEM((1024, 1024), bf16),
            pltpu.VMEM((1024, 2048), bf16),
            pltpu.VMEM((2048, 1024), bf16),
            pltpu.VMEM((ROWS, 1024), f32),
            pltpu.VMEM((PACK * CAP, ROWS), bf16),
            pltpu.VMEM((ROWS, PACK * CAP), bf16),
            pltpu.VMEM((ROWS, LANES), f32),
            pltpu.VMEM((PACK * CAP, 1024), bf16),
            pltpu.VMEM((PACK * CAP, 1024), bf16),
            pltpu.VMEM((ROWS, 2048), bf16),
            pltpu.VMEM((PACK * CAP, 1024), bf16),
            pltpu.VMEM((PACK * CAP, 1024), bf16),
            dma((7,)),
            dma((4,)),
            dma((4,)),
            dma((2, 2)),
            dma((2, 2)),
            dma((4 * KEPT,)),
            dma((4 * KEPT,)),
            dma((2 * PAIRS,)),
            dma((2 * PAIRS,)),
            dma((PAIRS - KEPT,)),
            dma((PAIRS - KEPT,)),
            dma((PACK,)),
            dma((PACK,)),
            dma((PACK,)),
            dma((PACK,)),
        ],
        compiler_params=pltpu.CompilerParams(
            collective_id=0, has_side_effects=True, vmem_limit_bytes=56 << 20
        ),
        name="layer",
    )(
        queries, keys, values, residual,
        row(segments), row(routes), row(gate_prob), row(norm_gain),
        out_weight, expert_in, expert_out,
    )


def solution(mesh):
    placed = (
        P(("dp", "pack"), None),
        P(("dp", "pack"), None),
        P(("dp", "pack"), None),
        P(("dp", "pack"), None),
        P(("dp", "pack")),
        P(),
        P(),
        P(("dp", "pack"), None),
        P(("dp", "pack")),
        P("pack", None, None),
        P("pack", None, None),
    )
    return jax.shard_map(
        on_device, mesh=mesh, in_specs=placed, out_specs=P(("dp", "pack"), None), check_vma=False
    )
```

```python
import jax
import jax.numpy as jnp
from jax import lax
from jax.experimental import pallas as pl
from jax.experimental.pallas import tpu as pltpu
from jax.sharding import PartitionSpec as P

HEADS = 16
PACK = 32
SIDE = 4
ROWS = 256
CAP = 16
PAIRS = HEADS // 2
LANES = 128
FAR_AWAY = -1e30
MESH = pl.DeviceIdType.MESH
OWN, SIB, NEAR, FAR, FWD = range(5)
KEPT = 5
WAVES = (0, 8, 19, 27, 32)
WIDE = 1024
AHEAD = 1
PICK_ORDER = (0, 1, 6, 2, 3, 7, 4, 5, 8, 9)
UNITS = tuple(("part", pair) for pair in range(PAIRS)) + (
    ("help", 5), ("home", 5), ("home", 0), ("help", 6), ("home", 6), ("home", 1),
    ("help", 7), ("home", 7), ("home", 2), ("home", 3), ("home", 4),
)


def hops(step):
    return min(step[0], SIDE - step[0]) + min(step[1], SIDE - step[1])


STEPS = sorted(
    [(dy, dx, dc) for dy in range(SIDE) for dx in range(SIDE) for dc in (1, 0)],
    key=lambda step: (-hops(step), step[0], step[1], -step[2]),
)
HALF = PACK // 2


def moved(me, step, sign):
    y, x, core = me // (2 * SIDE), (me // 2) % SIDE, me % 2
    y = lax.rem(y + sign * step[0] + SIDE, SIDE)
    x = lax.rem(x + sign * step[1] + SIDE, SIDE)
    core = lax.rem(core + step[2], 2)
    return (y * SIDE + x) * 2 + core


def kernel(
    q_hbm, k_hbm, v_hbm, res_hbm, seg_ref, route_ref, gate_ref, gain_ref, wo_hbm, w1_hbm, w2_hbm,
    out_hbm,
    qs, kt, vt, near, fwd, pick, help_out, help_in, held_a, held_b, tops_a, tops_b, parts, part_tops,
    segs, qaug, kaug, helped, att,
    res, wo, w1, w2, stream, done, place, place_t, gate_cols, outg, recv, hid, prod, ret,
    load_sem, out_sem, seg_send, seg_recv, sib_send, sib_recv, near_send, near_recv, fwd_send, fwd_recv,
    help_send, help_recv, go_send, go_recv, back_send, back_recv,
):
    me = lax.axis_index("pack")
    core = lax.rem(me, 2)
    sibling = me + 1 - 2 * core
    across = lax.rem(me + 2 * core + PACK - 1, PACK)

    barrier = pltpu.get_barrier_semaphore()

    @pl.loop(1, PACK)
    def _(d):
        pl.semaphore_signal(
            barrier, inc=1, device_id={"pack": lax.rem(me + d, PACK)}, device_id_type=MESH
        )

    loads = [
        pltpu.make_async_copy(src, dst, load_sem.at[i])
        for i, (src, dst) in enumerate(
            [
                (k_hbm, kt.at[OWN]),
                (v_hbm, vt.at[OWN]),
                (q_hbm, qs),
                (res_hbm, res),
                (wo_hbm, wo),
                (w1_hbm.at[0], w1),
                (w2_hbm.at[0], w2),
            ]
        )
    ]
    for load in loads[:4]:
        load.start()
    segs[OWN] = jnp.broadcast_to(seg_ref[0:1, :], (8, ROWS))
    pl.semaphore_wait(barrier, PACK - 1)

    def cols(p):
        return pl.ds(pl.multiple_of(p * LANES, LANES), LANES)

    def remote(src, dst, send, recv_s, peer):
        return pltpu.make_async_remote_copy(
            src_ref=src, dst_ref=dst, send_sem=send, recv_sem=recv_s,
            device_id={"pack": peer}, device_id_type=MESH,
        )

    def plain(p):
        return [
            remote(hbm.at[:, cols(p)], near.at[2 * p + i], near_send.at[2 * p + i], near_recv.at[2 * p + i], across)
            for i, hbm in enumerate((k_hbm, v_hbm))
        ]

    def picked(n):
        at = 2 * KEPT + n
        return remote(pick.at[n], near.at[at], near_send.at[at], near_recv.at[at], across)

    def forward(n):
        return remote(near.at[n], fwd.at[n], fwd_send.at[n], fwd_recv.at[n], sibling)

    def helping(n):
        return remote(help_out.at[n], help_in.at[n], help_send.at[n], help_recv.at[n], across)

    seg_out = [
        remote(segs.at[OWN], segs.at[NEAR], seg_send.at[0], seg_recv.at[0], across),
        remote(segs.at[OWN], segs.at[SIB], seg_send.at[1], seg_recv.at[1], sibling),
    ]
    seg_on = [
        remote(segs.at[SIB], segs.at[FAR], seg_send.at[2], seg_recv.at[2], across),
        remote(segs.at[NEAR], segs.at[FWD], seg_send.at[3], seg_recv.at[3], sibling),
    ]
    first, rest = pl.ds(0, KEPT * LANES), pl.ds(KEPT * LANES, (PAIRS - KEPT) * LANES)
    sib_out = [
        remote(hbm.at[:, c], tile.at[SIB, :, c], sib_send.at[i, n], sib_recv.at[i, n], sibling)
        for n, c in enumerate((first, rest))
        for i, (hbm, tile) in enumerate(((k_hbm, kt), (v_hbm, vt)))
    ]
    for copy in seg_out + plain(0) + sib_out + plain(1):
        copy.start()

    expert_of = jnp.zeros((PACK, ROWS), jnp.int32)
    place_iota = lax.broadcasted_iota(jnp.int32, (PACK, ROWS), 0)
    for j, step in enumerate(STEPS):
        expert_of = jnp.where(place_iota == j, moved(me, step, 1), expert_of)
    chosen = jnp.broadcast_to(route_ref[0:1, :], (PACK, ROWS)) == expert_of
    earlier = lax.broadcasted_iota(jnp.int32, (ROWS, ROWS), 0) < lax.broadcasted_iota(
        jnp.int32, (ROWS, ROWS), 1
    )
    rank = jnp.dot(
        jnp.where(chosen, 1.0, 0.0).astype(jnp.bfloat16),
        jnp.where(earlier, 1.0, 0.0).astype(jnp.bfloat16),
        preferred_element_type=jnp.float32,
    )
    slot = jnp.where(chosen, rank, -1.0)
    slot_iota = lax.broadcasted_iota(jnp.int32, (CAP, ROWS), 0).astype(jnp.float32)
    for j in range(PACK):
        hit = jnp.broadcast_to(slot[j : j + 1, :], (CAP, ROWS)) == slot_iota
        hit = jnp.where(hit, 1.0, 0.0)
        place[CAP * j : CAP * (j + 1), :] = hit.astype(jnp.bfloat16)
    for j in range(0, PACK * CAP, LANES):
        place_t[:, j : j + LANES] = place[j : j + LANES, :].astype(jnp.float32).T.astype(jnp.bfloat16)
    gate_cols[...] = jnp.broadcast_to(gate_ref[0:1, :], (LANES, ROWS)).T

    def edge(row, at_end):
        return jnp.where(at_end, row[:, ROWS - 1 :], row[:, :1])

    for copy in seg_out:
        copy.wait_recv()
    for copy in seg_on:
        copy.start()
    for load in loads[:4]:
        load.wait()
    for copy in sib_out[:2]:
        copy.wait_recv()
    last = core == 1
    sib_edge = edge(segs[SIB, 0:1, :], last)
    near_edge = edge(segs[NEAR, 0:1, :], core == 0)
    own_edge = edge(segs[OWN, 0:1, :], last)
    wide_here = jnp.broadcast_to(sib_edge, (ROWS, LANES)) == jnp.broadcast_to(near_edge, (ROWS, LANES))
    usual = [(t.at[OWN], p) for p in range(KEPT, PAIRS) for t in (kt, vt)]
    usual += [(qs, p) for p in range(KEPT, PAIRS)]
    for n in range(2 * KEPT):
        wide = (kt, vt)[n % 2][SIB, :, LANES * (n // 2) : LANES * (n // 2 + 1)]
        if n < len(usual):
            src, p = usual[n]
            wide = jnp.where(wide_here, wide, src[:, LANES * p : LANES * (p + 1)])
        pick[n] = wide

    for n in PICK_ORDER:
        picked(n).start()

    @pl.loop(2, KEPT)
    def _(p):
        for copy in plain(p):
            copy.start()

    for load in loads[4:]:
        load.start()

    def image_rows(seg):
        spread = jnp.broadcast_to(seg[0:1, :], (LANES, ROWS))
        return spread == lax.broadcasted_iota(jnp.int32, (LANES, ROWS), 0)

    def query_marks(rows):
        return jnp.where(rows, FAR_AWAY, 0.0).T.astype(jnp.bfloat16)

    def key_marks(rows):
        return jnp.where(rows, 0.0, 1.0).T.astype(jnp.bfloat16)

    own_rows, near_rows = image_rows(segs[OWN]), image_rows(segs[NEAR])
    qaug[0] = query_marks(own_rows)
    qaug[1] = query_marks(near_rows)
    kaug[OWN] = key_marks(own_rows)
    kaug[NEAR] = key_marks(near_rows)
    kaug[SIB] = key_marks(image_rows(segs[SIB]))
    exp_scale = float((1024 // HEADS) ** -0.5 * 1.4426950408889634)
    low_lanes = lax.broadcasted_iota(jnp.int32, (ROWS, LANES), 1) < LANES // 2
    ones = jnp.ones((ROWS, LANES), jnp.bfloat16)

    def at_home(p, place_of):
        c = slice(p * LANES, (p + 1) * LANES)
        return (lambda: kt[place_of, :, c], lambda: kaug[place_of], lambda: vt[place_of, :, c])

    def arrived(buf, at, place_of):
        return (lambda: buf[at], lambda: kaug[place_of], lambda: buf[at + 1])

    def tiles_of(kind, p):
        here = [at_home(p, OWN), at_home(p, SIB)]
        if kind == "part":
            return here
        tiles = [arrived(near, 2 * p, NEAR)]
        if kind == "help":
            return here + tiles
        tiles.append(arrived(fwd, 2 * p, FWD))
        if p < KEPT:
            tiles.append(arrived(near, 2 * KEPT + 2 * p, FAR))
        return tiles

    def begin_unit(kind, p, held, tops):
        if kind != "help":
            both, marks = qs[:, p * LANES : (p + 1) * LANES], qaug[0]
        else:
            both, marks = near[2 * PAIRS + p - KEPT], qaug[1]
        zero = jnp.zeros_like(both)
        lhs = jnp.concatenate(
            [
                jnp.concatenate([jnp.where(low_lanes, both, zero), marks], axis=1),
                jnp.concatenate([jnp.where(low_lanes, zero, both), marks], axis=1),
            ],
            axis=0,
        )
        top = None
        for n, (key, mark, _) in enumerate(tiles_of(kind, p)):
            scores = lax.dot_general(
                lhs,
                jnp.concatenate([key(), mark()], axis=1),
                (((1,), (1,)), ((), ())),
                preferred_element_type=jnp.float32,
            )
            held[n] = scores
            top = scores if top is None else jnp.maximum(top, scores)
        top = jnp.broadcast_to(jnp.max(top, axis=1, keepdims=True), (2 * ROWS, LANES))
        if kind == "home":
            top = jnp.maximum(top, part_tops[p])
        tops[...] = top

    def finish_unit(kind, p, held, tops):
        top = jnp.concatenate([tops[...], tops[...]], axis=1)
        summed = jnp.zeros((2 * ROWS, 2 * LANES), jnp.float32)
        if kind == "home":
            shrink = jnp.exp2((part_tops[p] - tops[...]) * exp_scale)
            summed = parts[p] * jnp.concatenate([shrink, shrink], axis=1)
        for n, (_, _, value) in enumerate(tiles_of(kind, p)):
            weights = jnp.exp2((held[n] - top) * exp_scale).astype(jnp.bfloat16)
            rhs = jnp.concatenate([value(), ones], axis=1)
            summed = summed + jnp.dot(weights, rhs, preferred_element_type=jnp.float32)
        if kind == "part":
            parts[p] = summed
            part_tops[p] = tops[...]
            return
        both = summed[:, :LANES] / summed[:, LANES:]
        attended = jnp.where(low_lanes, both[:ROWS], both[ROWS:]).astype(jnp.bfloat16)
        if kind == "help":
            help_out[p - KEPT] = attended
            helping(p - KEPT).start()
        else:
            att[:, p * LANES : (p + 1) * LANES] = attended

    came = set()

    def near_came(at):
        if at not in came:
            came.add(at)
            copy = plain(at // 2)[at % 2] if at < 2 * KEPT else picked(at - 2 * KEPT)
            copy.wait_recv()
            if at < 2 * PAIRS:
                forward(at).start()

    def unit_came(kind, p):
        if kind == "part":
            return
        near_came(2 * p)
        near_came(2 * p + 1)
        if kind == "help":
            near_came(2 * PAIRS + p - KEPT)
        elif p < KEPT:
            near_came(2 * KEPT + 2 * p)
            near_came(2 * KEPT + 2 * p + 1)

    def marks_of_two_hops():
        for copy in seg_on:
            copy.wait_recv()
        kaug[FWD] = key_marks(image_rows(segs[FWD]))
        far_edge = edge(segs[FAR, 0:1, :], core == 0)
        wide_there = jnp.broadcast_to(far_edge, (LANES, ROWS)) == jnp.broadcast_to(own_edge, (LANES, ROWS))
        kaug[FAR] = key_marks(jnp.logical_and(wide_there, image_rows(segs[FAR])))
        in_crossing = jnp.broadcast_to(segs[OWN, 0:1, :], (LANES, ROWS)) == jnp.broadcast_to(own_edge, (LANES, ROWS))
        helped[...] = jnp.where(jnp.logical_and(wide_there, in_crossing), 1.0, 0.0).T

    for copy in sib_out[2:]:
        copy.wait_recv()
    stages = ((held_a, tops_a), (held_b, tops_b))
    for n, unit in enumerate(UNITS):
        if n == 4:
            for at in range(4):
                near_came(at)
        for later in UNITS[n : n + 1 + AHEAD]:
            unit_came(*later)
        if n == PAIRS:
            marks_of_two_hops()
        if unit[0] == "home":
            forward(2 * unit[1]).wait_recv()
            forward(2 * unit[1] + 1).wait_recv()
        begin_unit(*unit, *stages[n % 2])
        if n:
            finish_unit(*UNITS[n - 1], *stages[(n - 1) % 2])
    finish_unit(*UNITS[-1], *stages[(len(UNITS) - 1) % 2])

    loads[4].wait()
    kept = KEPT * LANES
    stream[...] = res[...].astype(jnp.float32) + jnp.dot(
        att[:, :kept], wo[:kept, :], preferred_element_type=jnp.float32
    )
    for n in range(PAIRS - KEPT):
        helping(n).wait_recv()
        c = slice((KEPT + n) * LANES, (KEPT + n + 1) * LANES)
        att[:, c] = jnp.where(helped[...] > 0.5, help_in[n], att[:, c])

    x = stream[...] + jnp.dot(
        att[:, KEPT * LANES :], wo[KEPT * LANES :, :], preferred_element_type=jnp.float32
    )
    stream[...] = x
    mean = jnp.mean(x, axis=1, keepdims=True)
    centered = x - mean
    var = jnp.mean(centered * centered, axis=1, keepdims=True)
    normed = (centered * lax.rsqrt(var + 1e-6) * gain_ref[0:1, :]).astype(jnp.bfloat16)

    def block(j):
        return pl.ds(j * CAP, CAP)

    go = [
        remote(outg.at[block(j)], recv.at[block(j)], go_send.at[j], go_recv.at[j], moved(me, step, 1))
        for j, step in enumerate(STEPS[:-1])
    ]
    back = [
        remote(prod.at[block(j)], ret.at[block(j)], back_send.at[j], back_recv.at[j], moved(me, step, -1))
        for j, step in enumerate(STEPS[:-1])
    ]
    part = 128
    for start in range(0, PACK * CAP, part):
        outg[start : start + part, :] = jnp.dot(
            place[start : start + part, :], normed, preferred_element_type=jnp.float32
        ).astype(jnp.bfloat16)
        for j in range(start // CAP, min((start + part) // CAP, PACK - 1)):
            go[j].start()
    recv[(PACK - 1) * CAP :, :] = outg[(PACK - 1) * CAP :, :]

    loads[5].wait()
    loads[6].wait()

    for begin, end in zip(WAVES, WAVES[1:]):
        rows, count = pl.ds(begin * CAP, (end - begin) * CAP), (end - begin) * CAP
        for j in range(begin, min(end, PACK - 1)):
            go[j].wait_recv()

        @pl.loop(0, 2048 // WIDE)
        def _(n):
            c = pl.ds(pl.multiple_of(n * WIDE, WIDE), WIDE)
            h = jnp.dot(recv[rows, :], w1[:, c], preferred_element_type=jnp.float32)
            h = 0.5 * h * (1.0 + lax.erf(h * 0.7071067811865476))
            hid[:count, c] = h.astype(jnp.bfloat16)

        @pl.loop(0, 1024 // WIDE)
        def _(n):
            c = pl.ds(pl.multiple_of(n * WIDE, WIDE), WIDE)
            prod[rows, c] = jnp.dot(
                hid[:count, :], w2[:, c], preferred_element_type=jnp.float32
            ).astype(jnp.bfloat16)

        for j in range(begin, min(end, PACK - 1)):
            back[j].start()
    ret[(PACK - 1) * CAP :, :] = prod[(PACK - 1) * CAP :, :]

    gate = jnp.concatenate([gate_cols[...]] * (1024 // LANES), axis=1)
    for j in range(HALF):
        back[j].wait_recv()
    stream[...] += gate * jnp.dot(place_t[:, :ROWS], ret[:ROWS, :], preferred_element_type=jnp.float32)
    for j in range(HALF, PACK - 1):
        back[j].wait_recv()
    upper = ROWS // 2
    leaving = []
    for n in range(2):
        r = slice(n * upper, (n + 1) * upper)
        second = jnp.dot(place_t[r, ROWS:], ret[ROWS:, :], preferred_element_type=jnp.float32)
        done[r, :] = (stream[r, :] + gate[r, :] * second).astype(done.dtype)
        rows = pl.ds(n * upper, upper)
        leaving.append(pltpu.make_async_copy(done.at[rows], out_hbm.at[rows], out_sem.at[n]))
        leaving[n].start()

    for copy in seg_out + seg_on + sib_out:
        copy.wait_send()

    @pl.loop(0, KEPT)
    def _(p):
        for copy in plain(p):
            copy.wait_send()

    @pl.loop(0, 2 * KEPT)
    def _(n):
        picked(n).wait_send()

    @pl.loop(0, 2 * PAIRS)
    def _(n):
        forward(n).wait_send()

    for n in range(PAIRS - KEPT):
        helping(n).wait_send()
    for copy in go + back:
        copy.wait_send()
    for copy in leaving:
        copy.wait()


def on_device(
    queries, keys, values, residual, segments, out_weight, norm_gain, routes, gate_prob,
    expert_in, expert_out,
):
    bf16, f32 = jnp.bfloat16, jnp.float32
    hbm = pl.BlockSpec(memory_space=pl.ANY)
    vmem = pl.BlockSpec(memory_space=pltpu.VMEM)
    row = lambda vector: vector.reshape(1, -1)
    dma = pltpu.SemaphoreType.DMA
    return pl.pallas_call(
        kernel,
        out_shape=jax.ShapeDtypeStruct((ROWS, 1024), bf16),
        in_specs=[hbm] * 4 + [vmem] * 4 + [hbm] * 3,
        out_specs=hbm,
        scratch_shapes=[
            pltpu.VMEM((ROWS, 1024), bf16),
            pltpu.VMEM((2, ROWS, 1024), bf16),
            pltpu.VMEM((2, ROWS, 1024), bf16),
            pltpu.VMEM((4 * KEPT, ROWS, LANES), bf16),
            pltpu.VMEM((2 * PAIRS, ROWS, LANES), bf16),
            pltpu.VMEM((2 * KEPT, ROWS, LANES), bf16),
            pltpu.VMEM((PAIRS - KEPT, ROWS, LANES), bf16),
            pltpu.VMEM((PAIRS - KEPT, ROWS, LANES), bf16),
            pltpu.VMEM((3, 2 * ROWS, ROWS), f32),
            pltpu.VMEM((3, 2 * ROWS, ROWS), f32),
            pltpu.VMEM((2 * ROWS, LANES), f32),
            pltpu.VMEM((2 * ROWS, LANES), f32),
            pltpu.VMEM((PAIRS, 2 * ROWS, 2 * LANES), f32),
            pltpu.VMEM((PAIRS, 2 * ROWS, LANES), f32),
            pltpu.VMEM((5, 8, ROWS), jnp.int32),
            pltpu.VMEM((2, ROWS, LANES), bf16),
            pltpu.VMEM((5, ROWS, LANES), bf16),
            pltpu.VMEM((ROWS, LANES), f32),
            pltpu.VMEM((ROWS, 1024), bf16),
            pltpu.VMEM((ROWS, 1024), bf16),
            pltpu.VMEM((1024, 1024), bf16),
            pltpu.VMEM((1024, 2048), bf16),
            pltpu.VMEM((2048, 1024), bf16),
            pltpu.VMEM((ROWS, 1024), f32),
            pltpu.VMEM((ROWS, 1024), bf16),
            pltpu.VMEM((PACK * CAP, ROWS), bf16),
            pltpu.VMEM((ROWS, PACK * CAP), bf16),
            pltpu.VMEM((ROWS, LANES), f32),
            pltpu.VMEM((PACK * CAP, 1024), bf16),
            pltpu.VMEM((PACK * CAP, 1024), bf16),
            pltpu.VMEM((ROWS, 2048), bf16),
            pltpu.VMEM((PACK * CAP, 1024), bf16),
            pltpu.VMEM((PACK * CAP, 1024), bf16),
            dma((7,)),
            dma((2,)),
            dma((4,)),
            dma((4,)),
            dma((2, 2)),
            dma((2, 2)),
            dma((4 * KEPT,)),
            dma((4 * KEPT,)),
            dma((2 * PAIRS,)),
            dma((2 * PAIRS,)),
            dma((PAIRS - KEPT,)),
            dma((PAIRS - KEPT,)),
            dma((PACK,)),
            dma((PACK,)),
            dma((PACK,)),
            dma((PACK,)),
        ],
        compiler_params=pltpu.CompilerParams(
            collective_id=0, has_side_effects=True, vmem_limit_bytes=56 << 20
        ),
        name="layer",
    )(
        queries, keys, values, residual,
        row(segments), row(routes), row(gate_prob), row(norm_gain),
        out_weight, expert_in, expert_out,
    )


def solution(mesh):
    placed = (
        P(("dp", "pack"), None),
        P(("dp", "pack"), None),
        P(("dp", "pack"), None),
        P(("dp", "pack"), None),
        P(("dp", "pack")),
        P(),
        P(),
        P(("dp", "pack"), None),
        P(("dp", "pack")),
        P("pack", None, None),
        P("pack", None, None),
    )
    return jax.shard_map(
        on_device, mesh=mesh, in_specs=placed, out_specs=P(("dp", "pack"), None), check_vma=False
    )
```
